32 devices in a mesh: section: 4 (over z), dp: 8 (over y, x, core).
Axes of the slice: x: 2, y: 2, z: 4, core: 2. Of those that a mesh axis runs over, the one named last changes fastest.
Arguments:
- query_states: bfloat16 [4, 3584, 2048], P('section', 'dp'), may hold values from -400 to 400
- cache_emb: bfloat16 [32, 128, 896], P('dp'), may hold values from -6 to 6
- nb_owner: int32 [4, 56, 2], P('section', 'dp'), may hold values from 0 to 7, all different within a row; in each aligned block of 7 rows (0 to 6, 7 to 13, ..., all dimensions but the last counted through in order) at most 2 rows name the same one
- nb_row: int32 [4, 56, 2], P('section', 'dp'), may hold values from 0 to 3
- enc_gain: float32 [4, 896], P('section'), may hold values from 0.1 to 1.9
- w_qkv: bfloat16 [4, 896, 2688], P('section'), may hold values from -0.1875 to 0.1875
- w_out: bfloat16 [4, 896, 896], P('section'), may hold values from -0.1875 to 0.1875
- w_kv: bfloat16 [4, 896, 4096], P('section'), may hold values from -0.1875 to 0.1875
Outputs:
- cross_out: bfloat16 [4, 3584, 2048], P('section', 'dp')
The draws below stay inside these ranges and needn't reach their ends.
Inputs may be any that keep to these rules, and one draw needn't show every extreme that they name: `nb_owner`: the 2 neighbours of one span name different shards; among the spans of one device no shard is named more than 2 times.
All inputs are finite; a program needn't handle non-finite values.
Results may differ from the reference program's by a relative error of at most 0.019.
Values may be sent and summed in bfloat16 or wider, within the bound.
No kernel may reach another device: no remote copies, remote signals or barrier semaphores. Data moves between devices by JAX's collectives and lax.ppermute only.
A program may use at most 128 MiB of HBM per device.

```python
import math
import jax
import jax.numpy as jnp
import numpy as np
from jax import lax

HD = 128
HEADS_W = 16
ENC_HD = 64
SPAN = 64
NB = 2
NB_LEN = 128
CAP = 2
ROW_DEV = 4
CH_DEV = 7
HW = 2048
E = 896
SPANS = 56
TOKENS = 3584
ROWS = 32
SECTIONS = 4
N_SECTION = 4
N_DP = 8


def draw_query_states(key, part):
    return jnp.clip(jax.random.normal(key, (SECTIONS, TOKENS, HW), jnp.float32) * 2.0, -12.0, 12.0).astype(jnp.bfloat16)


def place_ends(drawn, stream_key, low, largest):
    extent = drawn.shape
    spot = [jax.random.randint(jax.random.fold_in(stream_key, axis), (), 0, extent[axis]) for axis in range(len(extent))]
    drawn = drawn.at[tuple(spot)].set(low)
    longest = extent.index(max(extent))
    spot[longest] = (spot[longest] + 1) % extent[longest]
    return drawn.at[tuple(spot)].set(largest)


def steps_of(rng, dims, split, smallest, high):
    gain = 1.0
    for position, shards_of in split:
        heights = jax.random.uniform(jax.random.fold_in(jax.random.fold_in(rng, 6), position), (shards_of,), jnp.float32, smallest / len(split), high / len(split))
        gain = gain * jnp.repeat(jnp.exp(heights), dims[position] // shards_of).reshape((-1,) + (1,) * (len(dims) - 1 - position))
    return gain


def shared_out(rng, own, number, rows, count, top, reach, lean):
    sequence = jax.random.permutation(rng, count)
    packed, usual = portions_of(count, rows * top, reach, lean, True), portions_of(count, rows * top, reach, lean, False)
    places = jnp.arange(count)

    def named(tallies, offset_by):
        used = int((tallies > 0).sum())
        fixed = max(1, used // 4)
        passed = fixed + (places - fixed + offset_by * (used - fixed)) % max(1, count - fixed)
        return jnp.zeros((count,), jnp.int32).at[sequence[jnp.where(places < fixed, places, passed)]].set(jnp.asarray(tallies, jnp.int32))

    tallies = jnp.where(number % 4 == 0, named(packed, number // 4), named(usual, number - number // 4 - 1))
    mixed = jax.random.permutation(jax.random.fold_in(own, 3), count)
    giver, sink = mixed[0:count // 2 * 2:2], mixed[1:count // 2 * 2:2]
    margin = jnp.minimum(tallies[giver] - 1, reach - tallies[sink]) // 2
    margin = jnp.where((giver == sequence[0]) | (sink == sequence[0]) | (tallies[sink] == 0), 0, jnp.maximum(margin, 0))
    passed = jax.random.randint(jax.random.fold_in(own, 4), (count // 2,), 0, 1 << 20) % (margin + 1)
    tallies = tallies.at[giver].add(-passed).at[sink].add(passed)
    items = jnp.searchsorted(jnp.cumsum(tallies), jnp.arange(rows * top), side="right").astype(jnp.int32)
    listing = items.reshape(top, rows).T
    listing = listing[jax.random.permutation(jax.random.fold_in(own, 1), rows)]
    offset_by = jax.random.randint(jax.random.fold_in(own, 2), (rows, 1), 0, top)
    return jnp.take_along_axis(listing, (jnp.arange(top)[None, :] + offset_by) % top, axis=1)


def portions_of(count, total, most, skew, full):
    portions = [(1 << 20) // math.isqrt(standing ** skew) + 1 for standing in range(1, count + 1)]
    largest = most if full else min(most, max(-(-total // count), total * portions[0] // sum(portions)))
    least = 1 if total - largest >= count - 1 else 0
    counts, rest = [largest] + [least] * (count - 1), total - largest - least * (count - 1)
    while rest > 0:
        free = [i for i in range(1, count) if counts[i] < largest] or [i for i in range(1, count) if counts[i] < most]
        whole, remaining = sum([portions[i] for i in free]), rest
        for i in free:
            more = min(most - counts[i], max(1, remaining * portions[i] // whole), rest)
            counts[i] = counts[i] + more
            rest = rest - more
    return np.array(counts)


def noise(rng, dims, width, most, shards=(), kind=jnp.bfloat16):
    result = width * jax.random.normal(rng, dims, jnp.float32)
    if shards:
        result = result * steps_of(rng, dims, shards, -0.22, 0.18)
    return jnp.clip(result, -most, most).astype(kind)


def setup_inputs(seed: int = 0) -> dict:
    seeds = jax.random.split(jax.random.key(seed), 9)
    query_states = draw_query_states(jax.random.fold_in(seeds[8], 71), 0)
    cache_emb = noise(seeds[1], (ROWS, NB_LEN, E), 1.0, 6.0, ((0, 8),))
    nb_owner_keys = jax.random.split(jax.random.fold_in(seeds[2], 1), SECTIONS * SPANS // CH_DEV)
    nb_owner_turns = jax.random.permutation(jax.random.fold_in(seeds[2], 3), SECTIONS * SPANS // CH_DEV)
    nb_owner = jax.vmap(lambda own, number: shared_out(jax.random.fold_in(seeds[2], 2), own, number, CH_DEV, N_DP, NB, CAP, 2))(nb_owner_keys, nb_owner_turns).reshape((SECTIONS, SPANS, NB))
    nb_row = place_ends(jax.random.randint(seeds[3], (SECTIONS, SPANS, NB), 0, ROW_DEV), jax.random.fold_in(seeds[3], 1), 0, ROW_DEV - 1).astype(jnp.int32)
    enc_gain = jnp.clip(1.0 + 0.18 * jax.random.normal(seeds[4], (SECTIONS, E), jnp.float32), 0.1, 1.9)
    w_qkv = noise(seeds[5], (SECTIONS, E, 3 * E), E ** -0.5, 0.1875, ((0, 4),))
    w_out = noise(seeds[6], (SECTIONS, E, E), E ** -0.5, 0.1875, ((0, 4),))
    w_kv = noise(seeds[7], (SECTIONS, E, 2 * HW), E ** -0.5, 0.1875, ((0, 4),))
    return dict(query_states=query_states, cache_emb=cache_emb, nb_owner=nb_owner, nb_row=nb_row, enc_gain=enc_gain, w_qkv=w_qkv, w_out=w_out, w_kv=w_kv)


def encode(tokens, norm_gain, w_qkv, w_out):
    neighbours, length, features = tokens.shape
    head_count = features // ENC_HD
    floats = tokens.astype(jnp.float32)
    factor = lax.rsqrt(lax.optimization_barrier(jnp.mean(floats * floats, axis=-1, keepdims=True)) + 1e-06)
    normed = (floats * factor * norm_gain).astype(jnp.bfloat16)
    projected = jnp.einsum('mte,ef->mtf', normed.astype(jnp.float32), w_qkv.astype(jnp.float32)).astype(jnp.bfloat16)
    enc_queries = projected[..., :features].reshape(neighbours, length, head_count, ENC_HD)
    enc_keys = projected[..., features:2 * features].reshape(neighbours, length, head_count, ENC_HD)
    enc_values = projected[..., 2 * features:].reshape(neighbours, length, head_count, ENC_HD)
    scores = jnp.einsum('mqhd,mkhd->mhqk', enc_queries.astype(jnp.float32), enc_keys.astype(jnp.float32)) / math.sqrt(ENC_HD)
    powers = jnp.exp(scores)
    weights = (powers / lax.optimization_barrier(jnp.sum(powers, axis=-1, keepdims=True))).astype(jnp.bfloat16)
    context = jnp.einsum('mhqk,mkhd->mqhd', weights.astype(jnp.float32), enc_values.astype(jnp.float32)).astype(jnp.bfloat16)
    context = context.reshape(neighbours, length, features)
    branch = jnp.einsum('mte,ef->mtf', context.astype(jnp.float32), w_out.astype(jnp.float32))
    return (floats + branch).astype(jnp.bfloat16)

def attend_block(tokens, queries, norm_gain, w_qkv, w_out, w_kv):
    encoded = encode(tokens, norm_gain, w_qkv, w_out)
    keyvals = jnp.einsum('mte,ef->mtf', encoded.astype(jnp.float32), w_kv.astype(jnp.float32)).astype(jnp.bfloat16)
    spans = queries.shape[0] // SPAN
    cross_keys = keyvals[..., :HW].reshape(spans, NB * NB_LEN, HEADS_W, HD)
    cross_values = keyvals[..., HW:].reshape(spans, NB * NB_LEN, HEADS_W, HD)
    grouped = queries.reshape(spans, SPAN, HEADS_W, HD)
    scores = jnp.einsum('cqhd,ckhd->chqk', grouped.astype(jnp.float32), cross_keys.astype(jnp.float32)) / math.sqrt(HD)
    highest = lax.optimization_barrier(jnp.max(scores, axis=-1, keepdims=True))
    powers = jnp.exp(scores - highest)
    weights = (powers / lax.optimization_barrier(jnp.sum(powers, axis=-1, keepdims=True))).astype(jnp.bfloat16)
    output = jnp.einsum('chqk,ckhd->cqhd', weights.astype(jnp.float32), cross_values.astype(jnp.float32)).astype(jnp.bfloat16)
    return output.reshape(spans * SPAN, HEADS_W * HD)

def reference(query_states, cache_emb, nb_owner, nb_row, enc_gain, w_qkv, w_out, w_kv):
    received = jnp.roll(query_states, 1, axis=0)
    results = []
    for section_index in range(N_SECTION):
        row_ids = (nb_owner[section_index] * ROW_DEV + nb_row[section_index]).astype(jnp.int32).reshape(N_DP, CH_DEV * NB)
        queries = received[section_index].reshape(N_DP, CH_DEV * SPAN, HW)
        section_gain = enc_gain[section_index]
        section_qkv = w_qkv[section_index]
        section_out = w_out[section_index]
        section_kv = w_kv[section_index]

        def one_block(pieces):
            block_ids, block_queries = pieces
            tokens = jnp.take(cache_emb, block_ids, axis=0)
            return attend_block(tokens, block_queries, section_gain, section_qkv, section_out, section_kv)
        stacked = lax.map(one_block, (row_ids, queries))
        results.append(stacked.reshape(TOKENS, HW))
    return jnp.stack(results)
```

```python
import functools
import math

import jax
import jax.numpy as jnp
from jax import lax
from jax.experimental import pallas as pl
from jax.experimental.pallas import tpu as pltpu
from jax.sharding import PartitionSpec as P

HD = 128
ENC_HD = 64
SPAN = 64
LOG2E = 1.4426950408889634
BF = jnp.bfloat16
F32 = jnp.float32
MB = 2**20
ANY = pl.BlockSpec(memory_space=pl.ANY)
VM = pl.BlockSpec(memory_space=pltpu.VMEM)
SM = pl.BlockSpec(memory_space=pltpu.SMEM)
EARLY = 5
E_US, KV_US, CROSS_US = 8.0, 4.0, 6.0


def cost(us):
    return pl.CostEstimate(flops=int(us * 1.0e9), bytes_accessed=1, transcendentals=0)


def encode_kernel(
    rows_ref, gain_ref, wqkv_hbm, wout_hbm, out_ref, wqkv, wout, proj, ctx, sems
):
    count, length, width = rows_ref.shape
    step = width // 4
    pieces = [
        [
            pltpu.make_async_copy(
                wqkv_hbm.at[0, pl.ds(j * step, step), pl.ds(i * width, width)],
                wqkv.at[pl.ds(j * step, step), pl.ds(i * width, width)],
                sems.at[4 * i + j],
            )
            for j in range(4)
        ]
        for i in range(3)
    ]
    last = pltpu.make_async_copy(wout_hbm.at[0], wout, sems.at[12])
    for piece in pieces:
        for copy in piece:
            copy.start()
    last.start()
    tokens = rows_ref[...].reshape(count * length, width)
    floats = tokens.astype(F32)
    factor = lax.rsqrt(jnp.mean(floats * floats, axis=-1, keepdims=True) + 1e-06)
    ctx[...] = (floats * factor * gain_ref[...]).astype(BF)
    for i, piece in enumerate(pieces):
        for copy in piece:
            copy.wait()
        cols = slice(i * width, (i + 1) * width)
        proj[:, cols] = jnp.dot(ctx[...], wqkv[:, cols], preferred_element_type=F32).astype(BF)
    lane = lax.broadcasted_iota(jnp.int32, (length, 2 * ENC_HD), 1)
    first = lane < ENC_HD
    zero = jnp.zeros((length, 2 * ENC_HD), BF)
    scale = LOG2E / math.sqrt(ENC_HD)
    column = lax.broadcasted_iota(jnp.int32, (2 * length, 2 * length), 1)
    line = lax.broadcasted_iota(jnp.int32, (2 * length, 2 * length), 0)
    same = jnp.where((column < length) == (line < length), 1.0, 0.0).astype(BF)
    pairs = width // (2 * ENC_HD)
    for r in range(count):
        spot = slice(r * length, (r + 1) * length)

        def split(base):
            both = proj[spot, base : base + 2 * ENC_HD]
            return jnp.concatenate([jnp.where(first, both, zero), jnp.where(first, zero, both)], axis=0)

        scores = []
        for p in range(pairs):
            base = p * 2 * ENC_HD
            q2 = proj[spot, base : base + 2 * ENC_HD]
            scores.append(
                lax.dot_general(q2, split(width + base), (((1,), (1,)), ((), ())), preferred_element_type=F32)
            )
        powers = [jnp.exp2(part * scale) for part in scores]
        sums = [jnp.dot(part.astype(BF), same, preferred_element_type=F32) for part in powers]
        weights = [(part * (1.0 / total)).astype(BF) for part, total in zip(powers, sums)]
        for p in range(pairs):
            base = p * 2 * ENC_HD
            out = jnp.dot(weights[p], split(2 * width + base), preferred_element_type=F32)
            ctx[spot, base : base + 2 * ENC_HD] = out.astype(BF)
    last.wait()
    branch = jnp.dot(ctx[...], wout[...], preferred_element_type=F32)
    floats = rows_ref[...].reshape(count * length, width).astype(F32)
    out_ref[...] = (floats + branch).astype(BF).reshape(count, length, width)


def encode(rows, gain, w_qkv, w_out):
    count, length, width = rows.shape
    tokens = count * length
    return pl.pallas_call(
        encode_kernel,
        out_shape=jax.ShapeDtypeStruct(rows.shape, BF),
        in_specs=[VM, VM, ANY, ANY],
        out_specs=VM,
        scratch_shapes=[
            pltpu.VMEM((width, 3 * width), BF),
            pltpu.VMEM((width, width), BF),
            pltpu.VMEM((tokens, 3 * width), BF),
            pltpu.VMEM((tokens, width), BF),
            pltpu.SemaphoreType.DMA((13,)),
        ],
        compiler_params=pltpu.CompilerParams(vmem_limit_bytes=52 * MB),
        cost_estimate=cost(E_US),
        name="encode_rows",
    )(rows, gain, w_qkv, w_out)


def gather_rows(plan, sources, owner_ref, row_ref, me, rows, slots, sems, taken):
    spans, picks = owner_ref.shape[1:]

    def look(s, found):
        owner = owner_ref[0, s // picks, lax.rem(s, picks)]
        row = row_ref[0, s // picks, lax.rem(s, picks)]
        if taken is not None:
            taken[s] = 0
        for source, test, place in plan(sources, owner, jnp.bitwise_xor(owner, me), row):

            @pl.when(test)
            def _():
                slots[found] = s
                if taken is not None:
                    taken[s] = 1
                pltpu.make_async_copy(source.at[place], rows.at[found], sems.at[found]).start()

            found = found + test.astype(jnp.int32)
        return found

    return lax.fori_loop(0, spans * picks, look, jnp.int32(0))


def project_pairs(found, source, w_ref, rows, sems, finish, after):
    length, width = rows.shape[1:]
    chunk = 1024

    def project(g, carry):
        i = 2 * g
        pltpu.make_async_copy(source.at[0], rows.at[i], sems.at[i]).wait()

        @pl.when(i + 1 < found)
        def _():
            pltpu.make_async_copy(source.at[0], rows.at[i + 1], sems.at[i + 1]).wait()

        both = rows[pl.ds(i, 2)].reshape(2 * length, width)
        for b in range(w_ref.shape[1] // chunk):
            cols = pl.ds(b * chunk, chunk)
            out = jnp.dot(both, w_ref[:, cols], preferred_element_type=F32).astype(BF)
            finish(i, cols, out[:length], out[length:])
        after(i)
        return carry

    lax.fori_loop(0, (found + 1) // 2, project, 0)


def kv_kernel(plan, n_src, fresh, *refs):
    owner_ref, row_ref, me_ref, w_in = refs[:4]
    sources = refs[4 : 4 + n_src]
    kv_hbm, w_ref, token_ref, rows, made, slots, sems, w_sem, out_sems = refs[-9:]
    if fresh:
        step = w_ref.shape[0] // 8
        loads = [
            pltpu.make_async_copy(w_in.at[0, pl.ds(i * step, step)], w_ref.at[pl.ds(i * step, step)], w_sem.at[i])
            for i in range(8)
        ]
        for load in loads:
            load.start()
    found = gather_rows(plan, sources, owner_ref, row_ref, me_ref[0], rows, slots, sems, None)
    if fresh:
        for load in loads:
            load.wait()

    def store(i):
        return pltpu.make_async_copy(made.at[i], kv_hbm.at[slots[i]], out_sems.at[i])

    def finish(i, cols, one, two):
        made[i, :, cols] = one
        made[i + 1, :, cols] = two

    def send(i):
        store(i).start()

        @pl.when(i + 1 < found)
        def _():
            store(i + 1).start()

    def drain(i, carry):
        store(i).wait()
        return carry

    project_pairs(found, sources[0], w_ref, rows, sems, finish, send)
    lax.fori_loop(0, found, drain, 0)
    token_ref[...] = jnp.zeros_like(token_ref)


def keyvals_part(owner, row, me, sources, w_kv, before, plan, most):
    length, width = sources[0].shape[1:]
    features = w_kv.shape[-1]
    slots = owner.shape[1] * owner.shape[2]
    most = min(most, slots)
    most += most % 2
    fresh = before is None
    operands = [owner, row, me, w_kv, *sources]
    specs = [SM, SM, SM, ANY if fresh else VM] + [ANY] * len(sources)
    aliases = {}
    if not fresh:
        aliases = {3: 1, len(operands): 0}
        operands.append(before)
        specs.append(ANY)
    return pl.pallas_call(
        functools.partial(kv_kernel, plan, len(sources), fresh),
        out_shape=[
            jax.ShapeDtypeStruct((slots, length, features), BF),
            pltpu.VMEM((width, features), BF),
            jax.ShapeDtypeStruct((8, 128), F32),
        ],
        in_specs=specs,
        out_specs=[ANY, VM, VM],
        input_output_aliases=aliases,
        scratch_shapes=[
            pltpu.VMEM((most, length, width), BF),
            pltpu.VMEM((most, length, features), BF),
            pltpu.SMEM((most,), jnp.int32),
            pltpu.SemaphoreType.DMA((most,)),
            pltpu.SemaphoreType.DMA((8,)),
            pltpu.SemaphoreType.DMA((most,)),
        ],
        compiler_params=pltpu.CompilerParams(vmem_limit_bytes=48 * MB),
        cost_estimate=cost(KV_US),
        name="keyvals_rows",
    )(*operands)


def attend_span(span, queries, kv_ref, out_ref):
    width = queries.shape[1]
    picks, length = 2, kv_ref.shape[1]
    keys = picks * length
    lane = lax.broadcasted_iota(jnp.int32, (SPAN, 2 * HD), 1)
    first = lane < HD
    zero = jnp.zeros((SPAN, 2 * HD), BF)
    scale = LOG2E / math.sqrt(HD)
    pairs = width // (2 * HD)
    here = pl.ds(pl.multiple_of(span * SPAN, SPAN), SPAN)
    scores = []
    for h in range(pairs):
        cols = slice(h * 2 * HD, (h + 1) * 2 * HD)
        q = queries[here, cols]
        qq = jnp.concatenate([jnp.where(first, q, zero), jnp.where(first, zero, q)], axis=0)
        k = kv_ref[pl.ds(span * picks, picks), :, cols].reshape(keys, 2 * HD)
        scores.append(lax.dot_general(qq, k, (((1,), (1,)), ((), ())), preferred_element_type=F32))
    weights = []
    for part in scores:
        highest = jnp.max(part, axis=-1, keepdims=True)
        powers = jnp.exp2((part - highest) * scale)
        weights.append((powers.astype(BF), 1.0 / jnp.sum(powers, axis=-1, keepdims=True)))
    for h in range(pairs):
        cols = slice(h * 2 * HD, (h + 1) * 2 * HD)
        values = slice(width + h * 2 * HD, width + (h + 1) * 2 * HD)
        v = kv_ref[pl.ds(span * picks, picks), :, values].reshape(keys, 2 * HD)
        both = jnp.dot(weights[h][0], v, preferred_element_type=F32) * weights[h][1]
        out_ref[here, cols] = jnp.where(first, both[:SPAN], both[SPAN:]).astype(BF)


def final_kernel(plan, n_src, *refs):
    owner_ref, row_ref, me_ref, w_ref, kv_hbm, first_hbm, second_hbm = refs[:7]
    sources = refs[7 : 7 + n_src]
    out_hbm, rows, keyvals, queries, result, slots, taken, sems, kv_sems, q_sems, out_sems = refs[7 + n_src :]
    cut = first_hbm.shape[1]
    tokens = queries.shape[0]
    picks = owner_ref.shape[2]
    total = owner_ref.shape[1] * picks
    found = gather_rows(plan, sources, owner_ref, row_ref, me_ref[0], rows, slots, sems, taken)
    loads = [
        pltpu.make_async_copy(first_hbm.at[0], queries.at[pl.ds(0, cut)], q_sems.at[0]),
        pltpu.make_async_copy(second_hbm.at[0], queries.at[pl.ds(cut, tokens - cut)], q_sems.at[1]),
    ]
    for load in loads:
        load.start()

    def fetch(s):
        return pltpu.make_async_copy(kv_hbm.at[s], keyvals.at[s], kv_sems.at[s])

    def begin(s, carry):
        @pl.when(taken[s] == 0)
        def _():
            fetch(s).start()

        return carry

    lax.fori_loop(0, total, begin, 0)

    def finish(i, cols, one, two):
        keyvals[slots[i], :, cols] = one

        @pl.when(i + 1 < found)
        def _():
            keyvals[slots[i + 1], :, cols] = two

    if n_src:
        project_pairs(found, sources[0], w_ref, rows, sems, finish, lambda i: None)
    for load in loads:
        load.wait()

    def store(span):
        here = pl.ds(pl.multiple_of(span * SPAN, SPAN), SPAN)
        return pltpu.make_async_copy(result.at[here], out_hbm.at[0, here], out_sems.at[span])

    def attend(span, carry):
        for j in range(picks):
            s = span * picks + j

            @pl.when(taken[s] == 0)
            def _():
                fetch(s).wait()

        attend_span(span, queries, keyvals, result)
        store(span).start()
        return carry

    lax.fori_loop(0, tokens // SPAN, attend, 0)

    def drain(span, carry):
        store(span).wait()
        return carry

    lax.fori_loop(0, tokens // SPAN, drain, 0)


def final(owner, row, me, sources, w, kv, first, second, plan, most):
    length, width = kv.shape[1], w.shape[0]
    slots = owner.shape[1] * owner.shape[2]
    tokens, features = first.shape[1] + second.shape[1], first.shape[2]
    return pl.pallas_call(
        functools.partial(final_kernel, plan, len(sources)),
        out_shape=jax.ShapeDtypeStruct((1, tokens, features), BF),
        in_specs=[SM, SM, SM, VM] + [ANY] * (3 + len(sources)),
        out_specs=ANY,
        scratch_shapes=[
            pltpu.VMEM((most, length, width), BF),
            pltpu.VMEM((slots, length, kv.shape[2]), BF),
            pltpu.VMEM((tokens, features), BF),
            pltpu.VMEM((tokens, features), BF),
            pltpu.SMEM((most,), jnp.int32),
            pltpu.SMEM((slots,), jnp.int32),
            pltpu.SemaphoreType.DMA((most,)),
            pltpu.SemaphoreType.DMA((slots,)),
            pltpu.SemaphoreType.DMA((2,)),
            pltpu.SemaphoreType.DMA((tokens // SPAN,)),
        ],
        compiler_params=pltpu.CompilerParams(vmem_limit_bytes=36 * MB),
        cost_estimate=cost(CROSS_US),
        name="attend_spans",
    )(owner, row, me, w, kv, first, second, *sources)


def head_kernel(q_ref, out_ref, sem):
    copy = pltpu.make_async_copy(q_ref.at[:, pl.ds(0, out_ref.shape[1])], out_ref, sem)
    copy.start()
    copy.wait()


def head(queries, count):
    return pl.pallas_call(
        head_kernel,
        out_shape=pltpu.VMEM((1, count, queries.shape[2]), BF),
        in_specs=[ANY],
        out_specs=VM,
        scratch_shapes=[pltpu.SemaphoreType.DMA],
        compiler_params=pltpu.CompilerParams(vmem_limit_bytes=56 * MB),
        cost_estimate=cost(1.0),
        name="first_queries",
    )(queries)


def split_kernel(start, x_ref, y_ref, q_ref, done_ref, token_ref, low_ref, high_ref, out_ref, x_out, y_out, sems):
    half = low_ref.shape[0]
    copies = [
        pltpu.make_async_copy(x_ref.at[pl.ds(0, half)], low_ref, sems.at[0]),
        pltpu.make_async_copy(y_ref.at[pl.ds(half, high_ref.shape[0])], high_ref, sems.at[1]),
        pltpu.make_async_copy(q_ref.at[:, pl.ds(start, out_ref.shape[1])], out_ref, sems.at[2]),
    ]
    for copy in copies:
        copy.start()
    for copy in copies:
        copy.wait()


def split(x, y, queries, start, received, token):
    _, tokens, width = queries.shape
    half = x.shape[0] // 2
    return pl.pallas_call(
        functools.partial(split_kernel, start),
        out_shape=[
            pltpu.VMEM((half,) + x.shape[1:], BF),
            pltpu.VMEM((y.shape[0] - half,) + x.shape[1:], BF),
            pltpu.VMEM((1, tokens - start, width), BF),
            jax.ShapeDtypeStruct(x.shape, BF),
            jax.ShapeDtypeStruct(y.shape, BF),
        ],
        in_specs=[ANY, ANY, ANY, ANY, VM],
        out_specs=[VM] * 3 + [ANY] * 2,
        input_output_aliases={0: 3, 1: 4},
        scratch_shapes=[pltpu.SemaphoreType.DMA((3,))],
        compiler_params=pltpu.CompilerParams(vmem_limit_bytes=24 * MB),
        cost_estimate=cost(1.0),
        name="next_sends",
    )(x, y, queries, received, token)


def relay_kernel(low_ref, high_ref, token_ref, low_out, high_out):
    pass


def relay(low, high, token):
    return pl.pallas_call(
        relay_kernel,
        out_shape=[jax.ShapeDtypeStruct(low.shape, BF), jax.ShapeDtypeStruct(high.shape, BF)],
        in_specs=[ANY, ANY, ANY],
        out_specs=[ANY, ANY],
        input_output_aliases={0: 0, 1: 1},
        cost_estimate=cost(0.1),
        name="after_rows",
    )(low, high, token)


def shifted(block):
    n = lax.axis_size("section")
    return lax.ppermute(block, "section", [((i - 1) % n, i) for i in range(n)])


def swapped(block, hop):
    n = lax.axis_size("dp")
    return lax.ppermute(block, "dp", [(i, i ^ hop) for i in range(n)])


def shards(query_states, cache_emb, nb_owner, nb_row, enc_gain, w_qkv, w_out, w_kv):
    dp = lax.axis_size("dp")
    slots = nb_owner.shape[1] * nb_owner.shape[2]
    per = cache_emb.shape[0]
    spans = nb_owner.shape[1]
    start = EARLY * spans // 7 * SPAN
    first = shifted(head(query_states, start))
    me = lax.axis_index("dp").astype(jnp.int32).reshape(1)
    own = encode(cache_emb, enc_gain, w_qkv, w_out)
    part = functools.partial(keyvals_part, nb_owner, nb_row, me)
    if dp == 8 and per % 2 == 0:
        half = per // 2
        x, y, near = swapped(own, 2), swapped(own, 4), swapped(own, 1)
        kv, w, token = part([own, near], w_kv, None, lambda src, owner, hop, row: [(src[i], hop == i, row) for i in range(2)], 4)
        xl, yh, rest, x, y = split(x, y, query_states, start, first, token)
        dl, dh, second = swapped(xl, 4), swapped(yh, 2), shifted(rest)
        xs, ys = swapped(x, 1), swapped(y, 1)
        kv, w, token = part(
            [x, xs, y, ys], w, kv, lambda src, owner, hop, row: [(src[i], hop == i + 2, row) for i in range(4)], 8
        )

        def last(src, owner, hop, row):
            lows = [(src[i], (hop == i + 6) & (row < half), row) for i in range(2)]
            return lows + [(src[i + 2], (hop == i + 6) & (row >= half), row - half) for i in range(2)]

        dl, dh = relay(dl, dh, token)
        sources = [dl, swapped(dl, 1), dh, swapped(dh, 1)]
    else:
        whole = lax.all_gather(own, "dp", axis=0, tiled=True)
        second = shifted(query_states[:, start:])
        kv, w, _ = part([whole], w_kv, None, lambda src, owner, hop, row: [(src[0], owner >= 0, owner * per + row)], slots)
        sources = []

        def last(src, owner, hop, row):
            return []

    return final(nb_owner, nb_row, me, sources, w, kv, first, second, last, 4)


def solution(mesh):
    placed = (
        P("section", "dp", None),
        P("dp", None, None),
        P("section", "dp", None),
        P("section", "dp", None),
        P("section", None),
        P("section", None, None),
        P("section", None, None),
        P("section", None, None),
    )
    return jax.shard_map(
        shards, mesh=mesh, in_specs=placed, out_specs=P("section", "dp", None), check_vma=False
    )
```

```python
import functools
import math

import jax
import jax.numpy as jnp
from jax import lax
from jax.experimental import pallas as pl
from jax.experimental.pallas import tpu as pltpu
from jax.sharding import PartitionSpec as P

HD = 128
ENC_HD = 64
SPAN = 64
LOG2E = 1.4426950408889634
BF = jnp.bfloat16
F32 = jnp.float32
MB = 2**20
ANY = pl.BlockSpec(memory_space=pl.ANY)
VM = pl.BlockSpec(memory_space=pltpu.VMEM)
SM = pl.BlockSpec(memory_space=pltpu.SMEM)
EARLY = 5
PER = 1024
E_US, KV_US, CROSS_US = 8.0, 4.0, 6.0


def cost(us):
    return pl.CostEstimate(flops=int(us * 1.0e9), bytes_accessed=1, transcendentals=0)


def encode_kernel(
    rows_ref, gain_ref, wqkv_hbm, wout_hbm, out_ref, wqkv, wout, proj, ctx, sems
):
    count, length, width = rows_ref.shape
    step = width // 4
    pieces = [
        [
            pltpu.make_async_copy(
                wqkv_hbm.at[0, pl.ds(j * step, step), pl.ds(i * width, width)],
                wqkv.at[pl.ds(j * step, step), pl.ds(i * width, width)],
                sems.at[4 * i + j],
            )
            for j in range(4)
        ]
        for i in range(3)
    ]
    last = pltpu.make_async_copy(wout_hbm.at[0], wout, sems.at[12])
    for piece in pieces:
        for copy in piece:
            copy.start()
    last.start()
    tokens = rows_ref[...].reshape(count * length, width)
    floats = tokens.astype(F32)
    factor = lax.rsqrt(jnp.mean(floats * floats, axis=-1, keepdims=True) + 1e-06)
    ctx[...] = (floats * factor * gain_ref[...]).astype(BF)
    for i, piece in enumerate(pieces):
        for copy in piece:
            copy.wait()
        cols = slice(i * width, (i + 1) * width)
        proj[:, cols] = jnp.dot(ctx[...], wqkv[:, cols], preferred_element_type=F32).astype(BF)
    lane = lax.broadcasted_iota(jnp.int32, (length, 2 * ENC_HD), 1)
    first = lane < ENC_HD
    zero = jnp.zeros((length, 2 * ENC_HD), BF)
    scale = LOG2E / math.sqrt(ENC_HD)
    column = lax.broadcasted_iota(jnp.int32, (2 * length, 2 * length), 1)
    line = lax.broadcasted_iota(jnp.int32, (2 * length, 2 * length), 0)
    same = jnp.where((column < length) == (line < length), 1.0, 0.0).astype(BF)
    pairs = width // (2 * ENC_HD)
    for r in range(count):
        spot = slice(r * length, (r + 1) * length)

        def split(base):
            both = proj[spot, base : base + 2 * ENC_HD]
            return jnp.concatenate([jnp.where(first, both, zero), jnp.where(first, zero, both)], axis=0)

        scores = []
        for p in range(pairs):
            base = p * 2 * ENC_HD
            q2 = proj[spot, base : base + 2 * ENC_HD]
            scores.append(
                lax.dot_general(q2, split(width + base), (((1,), (1,)), ((), ())), preferred_element_type=F32)
            )
        powers = [jnp.exp2(part * scale) for part in scores]
        sums = [jnp.dot(part.astype(BF), same, preferred_element_type=F32) for part in powers]
        weights = [(part * (1.0 / total)).astype(BF) for part, total in zip(powers, sums)]
        for p in range(pairs):
            base = p * 2 * ENC_HD
            out = jnp.dot(weights[p], split(2 * width + base), preferred_element_type=F32)
            ctx[spot, base : base + 2 * ENC_HD] = out.astype(BF)
    last.wait()
    branch = jnp.dot(ctx[...], wout[...], preferred_element_type=F32)
    floats = rows_ref[...].reshape(count * length, width).astype(F32)
    out_ref[...] = (floats + branch).astype(BF).reshape(count, length, width)


def encode(rows, gain, w_qkv, w_out):
    count, length, width = rows.shape
    tokens = count * length
    return pl.pallas_call(
        encode_kernel,
        out_shape=jax.ShapeDtypeStruct(rows.shape, BF),
        in_specs=[VM, VM, ANY, ANY],
        out_specs=VM,
        scratch_shapes=[
            pltpu.VMEM((width, 3 * width), BF),
            pltpu.VMEM((width, width), BF),
            pltpu.VMEM((tokens, 3 * width), BF),
            pltpu.VMEM((tokens, width), BF),
            pltpu.SemaphoreType.DMA((13,)),
        ],
        compiler_params=pltpu.CompilerParams(vmem_limit_bytes=58 * MB),
        cost_estimate=cost(E_US),
        name="encode_rows",
    )(rows, gain, w_qkv, w_out)


def gather_rows(plan, sources, ids_ref, me, rows, slots, sems, taken):

    def look(s, found):
        code = ids_ref[s]
        owner, row = lax.shift_right_logical(code, 10), jnp.bitwise_and(code, PER - 1)
        if taken is not None:
            taken[s] = 0
        for source, test, place in plan(sources, owner, jnp.bitwise_xor(owner, me), row):

            @pl.when(test)
            def _():
                slots[found] = s
                if taken is not None:
                    taken[s] = 1
                pltpu.make_async_copy(source.at[place], rows.at[found], sems.at[found]).start()

            found = found + test.astype(jnp.int32)
        return found

    return lax.fori_loop(0, ids_ref.shape[0], look, jnp.int32(0))


def project_pairs(found, source, w_ref, rows, sems, finish):
    length, width = rows.shape[1:]
    chunk = 1024

    def project(g, carry):
        i = 2 * g
        pltpu.make_async_copy(source.at[0], rows.at[i], sems.at[i]).wait()

        @pl.when(i + 1 < found)
        def _():
            pltpu.make_async_copy(source.at[0], rows.at[i + 1], sems.at[i + 1]).wait()

        both = rows[pl.ds(i, 2)].reshape(2 * length, width)
        for b in range(w_ref.shape[1] // chunk):
            cols = pl.ds(b * chunk, chunk)
            out = jnp.dot(both, w_ref[:, cols], preferred_element_type=F32).astype(BF)
            finish(i, cols, out[:length], out[length:])
        return carry

    lax.fori_loop(0, (found + 1) // 2, project, 0)


def kv_kernel(plan, n_src, fresh, *refs):
    ids_ref, me_ref, w_in = refs[:3]
    sources = refs[3 : 3 + n_src]
    kv_hbm, w_ref, token_ref, rows, made, slots, sems, w_sem, out_sems = refs[-9:]
    if fresh:
        step = w_ref.shape[0] // 8
        loads = [
            pltpu.make_async_copy(w_in.at[0, pl.ds(i * step, step)], w_ref.at[pl.ds(i * step, step)], w_sem.at[i])
            for i in range(8)
        ]
        for load in loads:
            load.start()
    found = gather_rows(plan, sources, ids_ref, me_ref[0], rows, slots, sems, None)
    if fresh:
        for load in loads:
            load.wait()

    def store(i):
        return pltpu.make_async_copy(made.at[i], kv_hbm.at[slots[i]], out_sems.at[i])

    def send(i, cols):
        pltpu.make_async_copy(made.at[i, :, cols], kv_hbm.at[slots[i], :, cols], out_sems.at[i]).start()

    def finish(i, cols, one, two):
        made[i, :, cols] = one
        made[i + 1, :, cols] = two
        send(i, cols)

        @pl.when(i + 1 < found)
        def _():
            send(i + 1, cols)

    def drain(i, carry):
        store(i).wait()
        return carry

    project_pairs(found, sources[0], w_ref, rows, sems, finish)
    lax.fori_loop(0, found, drain, 0)
    token_ref[...] = jnp.zeros_like(token_ref)


def keyvals_part(ids, me, sources, w_kv, before, plan, most):
    length, width = sources[0].shape[1:]
    features = w_kv.shape[-1]
    slots = ids.shape[0]
    most = min(most, slots)
    most += most % 2
    fresh = before is None
    operands = [ids, me, w_kv, *sources]
    specs = [SM, SM, ANY if fresh else VM] + [ANY] * len(sources)
    aliases = {}
    if not fresh:
        aliases = {2: 1, len(operands): 0}
        operands.append(before)
        specs.append(ANY)
    return pl.pallas_call(
        functools.partial(kv_kernel, plan, len(sources), fresh),
        out_shape=[
            jax.ShapeDtypeStruct((slots, length, features), BF),
            pltpu.VMEM((width, features), BF),
            pltpu.VMEM((8, 128), F32),
        ],
        in_specs=specs,
        out_specs=[ANY, VM, VM],
        input_output_aliases=aliases,
        scratch_shapes=[
            pltpu.VMEM((most, length, width), BF),
            pltpu.VMEM((most, length, features), BF),
            pltpu.SMEM((most,), jnp.int32),
            pltpu.SemaphoreType.DMA((most,)),
            pltpu.SemaphoreType.DMA((8,)),
            pltpu.SemaphoreType.DMA((most,)),
        ],
        compiler_params=pltpu.CompilerParams(vmem_limit_bytes=48 * MB),
        cost_estimate=cost(KV_US),
        name="keyvals_rows",
    )(*operands)


def attend_span(span, queries, kv_ref, out_ref):
    width = queries.shape[1]
    picks, length = 2, kv_ref.shape[1]
    keys = picks * length
    lane = lax.broadcasted_iota(jnp.int32, (SPAN, 2 * HD), 1)
    first = lane < HD
    zero = jnp.zeros((SPAN, 2 * HD), BF)
    scale = LOG2E / math.sqrt(HD)
    pairs = width // (2 * HD)
    here = pl.ds(pl.multiple_of(span * SPAN, SPAN), SPAN)
    scores = []
    for h in range(pairs):
        cols = slice(h * 2 * HD, (h + 1) * 2 * HD)
        q = queries[here, cols]
        qq = jnp.concatenate([jnp.where(first, q, zero), jnp.where(first, zero, q)], axis=0)
        k = kv_ref[pl.ds(span * picks, picks), :, cols].reshape(keys, 2 * HD)
        scores.append(lax.dot_general(qq, k, (((1,), (1,)), ((), ())), preferred_element_type=F32))
    weights = []
    for part in scores:
        highest = jnp.max(part, axis=-1, keepdims=True)
        powers = jnp.exp2((part - highest) * scale)
        weights.append((powers.astype(BF), 1.0 / jnp.sum(powers, axis=-1, keepdims=True)))
    for h in range(pairs):
        cols = slice(h * 2 * HD, (h + 1) * 2 * HD)
        values = slice(width + h * 2 * HD, width + (h + 1) * 2 * HD)
        v = kv_ref[pl.ds(span * picks, picks), :, values].reshape(keys, 2 * HD)
        both = jnp.dot(weights[h][0], v, preferred_element_type=F32) * weights[h][1]
        out_ref[here, cols] = jnp.where(first, both[:SPAN], both[SPAN:]).astype(BF)


def final_kernel(plan, n_src, *refs):
    ids_ref, me_ref, w_ref, kv_hbm, first_hbm, second_hbm = refs[:6]
    sources = refs[6 : 6 + n_src]
    out_hbm, rows, keyvals, queries, result, slots, taken, sems, kv_sems, q_sems, out_sems = refs[6 + n_src :]
    cut = first_hbm.shape[1]
    tokens = queries.shape[0]
    total = ids_ref.shape[0]
    picks = total * SPAN // tokens
    found = gather_rows(plan, sources, ids_ref, me_ref[0], rows, slots, sems, taken)
    loads = [
        pltpu.make_async_copy(first_hbm.at[0], queries.at[pl.ds(0, cut)], q_sems.at[0]),
        pltpu.make_async_copy(second_hbm.at[0], queries.at[pl.ds(cut, tokens - cut)], q_sems.at[1]),
    ]
    for load in loads:
        load.start()

    def fetch(s):
        return pltpu.make_async_copy(kv_hbm.at[s], keyvals.at[s], kv_sems.at[s])

    def begin(s, carry):
        @pl.when(taken[s] == 0)
        def _():
            fetch(s).start()

        return carry

    lax.fori_loop(0, total, begin, 0)

    def finish(i, cols, one, two):
        keyvals[slots[i], :, cols] = one

        @pl.when(i + 1 < found)
        def _():
            keyvals[slots[i + 1], :, cols] = two

    if n_src:
        project_pairs(found, sources[0], w_ref, rows, sems, finish)
    for load in loads:
        load.wait()

    def store(span):
        here = pl.ds(pl.multiple_of(span * SPAN, SPAN), SPAN)
        return pltpu.make_async_copy(result.at[here], out_hbm.at[0, here], out_sems.at[span])

    def attend(span, carry):
        for j in range(picks):
            s = span * picks + j

            @pl.when(taken[s] == 0)
            def _():
                fetch(s).wait()

        attend_span(span, queries, keyvals, result)
        store(span).start()
        return carry

    lax.fori_loop(0, tokens // SPAN, attend, 0)

    def drain(span, carry):
        store(span).wait()
        return carry

    lax.fori_loop(0, tokens // SPAN, drain, 0)


def final(ids, me, sources, w, kv, first, second, plan, most):
    length, width = kv.shape[1], w.shape[0]
    slots = ids.shape[0]
    tokens, features = first.shape[1] + second.shape[1], first.shape[2]
    return pl.pallas_call(
        functools.partial(final_kernel, plan, len(sources)),
        out_shape=jax.ShapeDtypeStruct((1, tokens, features), BF),
        in_specs=[SM, SM, VM] + [ANY] * (3 + len(sources)),
        out_specs=ANY,
        scratch_shapes=[
            pltpu.VMEM((most, length, width), BF),
            pltpu.VMEM((slots, length, kv.shape[2]), BF),
            pltpu.VMEM((tokens, features), BF),
            pltpu.VMEM((tokens, features), BF),
            pltpu.SMEM((most,), jnp.int32),
            pltpu.SMEM((slots,), jnp.int32),
            pltpu.SemaphoreType.DMA((most,)),
            pltpu.SemaphoreType.DMA((slots,)),
            pltpu.SemaphoreType.DMA((2,)),
            pltpu.SemaphoreType.DMA((tokens // SPAN,)),
        ],
        compiler_params=pltpu.CompilerParams(vmem_limit_bytes=36 * MB),
        cost_estimate=cost(CROSS_US),
        name="attend_spans",
    )(ids, me, w, kv, first, second, *sources)


def head_kernel(q_ref, out_ref, sems):
    count = sems.shape[0]
    step = out_ref.shape[1] // count
    copies = [
        pltpu.make_async_copy(q_ref.at[:, pl.ds(i * step, step)], out_ref.at[:, pl.ds(i * step, step)], sems.at[i])
        for i in range(count)
    ]
    for copy in copies:
        copy.start()
    for copy in copies:
        copy.wait()


def head(queries, count):
    return pl.pallas_call(
        head_kernel,
        out_shape=pltpu.VMEM((1, count, queries.shape[2]), BF),
        in_specs=[ANY],
        out_specs=VM,
        scratch_shapes=[pltpu.SemaphoreType.DMA((count // SPAN,))],
        compiler_params=pltpu.CompilerParams(vmem_limit_bytes=56 * MB),
        cost_estimate=cost(1.0),
        name="first_queries",
    )(queries)


def split_kernel(
    start, x_ref, y_ref, q_ref, done_ref, token_ref, low_ref, high_ref, out_ref, x_out, y_out, sems
):
    half = low_ref.shape[0]
    copies = [
        pltpu.make_async_copy(x_ref.at[pl.ds(0, half)], low_ref, sems.at[0]),
        pltpu.make_async_copy(y_ref.at[pl.ds(half, high_ref.shape[0])], high_ref, sems.at[1]),
        pltpu.make_async_copy(q_ref.at[:, pl.ds(start, out_ref.shape[1])], out_ref, sems.at[2]),
    ]
    for copy in copies:
        copy.start()
    for copy in copies:
        copy.wait()


def split(x, y, queries, start, received, token):
    _, tokens, width = queries.shape
    half = x.shape[0] // 2
    return pl.pallas_call(
        functools.partial(split_kernel, start),
        out_shape=[
            pltpu.VMEM((half,) + x.shape[1:], BF),
            pltpu.VMEM((y.shape[0] - half,) + x.shape[1:], BF),
            pltpu.VMEM((1, tokens - start, width), BF),
            jax.ShapeDtypeStruct(x.shape, BF),
            jax.ShapeDtypeStruct(y.shape, BF),
        ],
        in_specs=[ANY, ANY, ANY, ANY, VM],
        out_specs=[VM] * 3 + [ANY] * 2,
        input_output_aliases={0: 3, 1: 4},
        scratch_shapes=[pltpu.SemaphoreType.DMA((3,))],
        compiler_params=pltpu.CompilerParams(vmem_limit_bytes=24 * MB),
        cost_estimate=cost(1.0),
        name="next_sends",
    )(x, y, queries, received, token)


def relay_kernel(low_ref, high_ref, token_ref, low_out, high_out):
    pass


def relay(low, high, token):
    return pl.pallas_call(
        relay_kernel,
        out_shape=[jax.ShapeDtypeStruct(low.shape, BF), jax.ShapeDtypeStruct(high.shape, BF)],
        in_specs=[ANY, ANY, VM],
        out_specs=[ANY, ANY],
        input_output_aliases={0: 0, 1: 1},
        compiler_params=pltpu.CompilerParams(vmem_limit_bytes=MB),
        cost_estimate=cost(0.1),
        name="after_rows",
    )(low, high, token)


def shifted(block):
    n = lax.axis_size("section")
    return lax.ppermute(block, "section", [((i - 1) % n, i) for i in range(n)])


def swapped(block, hop):
    n = lax.axis_size("dp")
    return lax.ppermute(block, "dp", [(i, i ^ hop) for i in range(n)])


def shards(query_states, cache_emb, nb_owner, nb_row, enc_gain, w_qkv, w_out, w_kv):
    dp = lax.axis_size("dp")
    slots = nb_owner.shape[1] * nb_owner.shape[2]
    per = cache_emb.shape[0]
    spans = nb_owner.shape[1]
    start = EARLY * spans // 7 * SPAN
    first = shifted(head(query_states, start))
    me = lax.axis_index("dp").astype(jnp.int32).reshape(1)
    ids = (nb_owner * PER + nb_row).reshape(-1)
    own = encode(cache_emb, enc_gain, w_qkv, w_out)
    part = functools.partial(keyvals_part, ids, me)
    if dp == 8 and per % 2 == 0:
        half = per // 2

        def nearest(src, owner, hop, row):
            return [(src[i], hop == i, row) for i in range(2)]

        def middle(src, owner, hop, row):
            return [(src[i], hop == i + 2, row) for i in range(4)]

        def last(src, owner, hop, row):
            lows = [(src[i], (hop == i + 6) & (row < half), row) for i in range(2)]
            return lows + [(src[i + 2], (hop == i + 6) & (row >= half), row - half) for i in range(2)]

        x, y, near = swapped(own, 2), swapped(own, 4), swapped(own, 1)
        kv, w, token = part([own, near], w_kv, None, nearest, 4)
        xl, yh, rest, x, y = split(x, y, query_states, start, first, token)
        dl, dh, second = swapped(xl, 4), swapped(yh, 2), shifted(rest)
        kv, w, token = part([x, swapped(x, 1), y, swapped(y, 1)], w, kv, middle, 8)
        dl, dh = relay(dl, dh, token)
        sources = [dl, swapped(dl, 1), dh, swapped(dh, 1)]
    else:
        whole = lax.all_gather(own, "dp", axis=0, tiled=True)
        second = shifted(query_states[:, start:])
        kv, w, _ = part([whole], w_kv, None, lambda src, owner, hop, row: [(src[0], owner >= 0, owner * per + row)], slots)
        sources = []

        def last(src, owner, hop, row):
            return []

    return final(ids, me, sources, w, kv, first, second, last, 4)


def solution(mesh):
    placed = (
        P("section", "dp", None),
        P("dp", None, None),
        P("section", "dp", None),
        P("section", "dp", None),
        P("section", None),
        P("section", None, None),
        P("section", None, None),
        P("section", None, None),
    )
    return jax.shard_map(
        shards, mesh=mesh, in_specs=placed, out_specs=P("section", "dp", None), check_vma=False
    )
```

```python
import functools
import math

import jax
import jax.numpy as jnp
from jax import lax
from jax.experimental import pallas as pl
from jax.experimental.pallas import tpu as pltpu
from jax.sharding import PartitionSpec as P

HD = 128
ENC_HD = 64
SPAN = 64
LOG2E = 1.4426950408889634
BF = jnp.bfloat16
F32 = jnp.float32
MB = 2**20
ANY = pl.BlockSpec(memory_space=pl.ANY)
VM = pl.BlockSpec(memory_space=pltpu.VMEM)
SM = pl.BlockSpec(memory_space=pltpu.SMEM)
PER = 1024
GROUP = 4
AHEAD = 3
E_US, KV_US, CROSS_US = 8.0, 4.0, 6.0


def cost(us):
    return pl.CostEstimate(flops=int(us * 1.0e9), bytes_accessed=1, transcendentals=0)


def encode_kernel(
    rows_ref, gain_ref, wqkv_hbm, wout_hbm, out_ref, wqkv, wout, proj, ctx, sems
):
    count, length, width = rows_ref.shape
    step = width // 4
    pieces = [
        [
            pltpu.make_async_copy(
                wqkv_hbm.at[0, pl.ds(j * step, step), pl.ds(i * width, width)],
                wqkv.at[pl.ds(j * step, step), pl.ds(i * width, width)],
                sems.at[4 * i + j],
            )
            for j in range(4)
        ]
        for i in range(3)
    ]
    last = pltpu.make_async_copy(wout_hbm.at[0], wout, sems.at[12])
    for piece in pieces:
        for copy in piece:
            copy.start()
    last.start()
    tokens = rows_ref[...].reshape(count * length, width)
    floats = tokens.astype(F32)
    factor = lax.rsqrt(jnp.mean(floats * floats, axis=-1, keepdims=True) + 1e-06)
    ctx[...] = (floats * factor * gain_ref[...]).astype(BF)
    for i, piece in enumerate(pieces):
        for copy in piece:
            copy.wait()
        cols = slice(i * width, (i + 1) * width)
        proj[:, cols] = jnp.dot(ctx[...], wqkv[:, cols], preferred_element_type=F32).astype(BF)
    lane = lax.broadcasted_iota(jnp.int32, (length, 2 * ENC_HD), 1)
    first = lane < ENC_HD
    zero = jnp.zeros((length, 2 * ENC_HD), BF)
    scale = LOG2E / math.sqrt(ENC_HD)
    column = lax.broadcasted_iota(jnp.int32, (2 * length, 2 * length), 1)
    line = lax.broadcasted_iota(jnp.int32, (2 * length, 2 * length), 0)
    same = jnp.where((column < length) == (line < length), 1.0, 0.0).astype(BF)
    pairs = width // (2 * ENC_HD)
    for r in range(count):
        spot = slice(r * length, (r + 1) * length)

        def split(base):
            both = proj[spot, base : base + 2 * ENC_HD]
            return jnp.concatenate([jnp.where(first, both, zero), jnp.where(first, zero, both)], axis=0)

        scores = []
        for p in range(pairs):
            base = p * 2 * ENC_HD
            q2 = proj[spot, base : base + 2 * ENC_HD]
            scores.append(
                lax.dot_general(q2, split(width + base), (((1,), (1,)), ((), ())), preferred_element_type=F32)
            )
        powers = [jnp.exp2(part * scale) for part in scores]
        sums = [jnp.dot(part.astype(BF), same, preferred_element_type=F32) for part in powers]
        weights = [(part * (1.0 / total)).astype(BF) for part, total in zip(powers, sums)]
        for p in range(pairs):
            base = p * 2 * ENC_HD
            out = jnp.dot(weights[p], split(2 * width + base), preferred_element_type=F32)
            ctx[spot, base : base + 2 * ENC_HD] = out.astype(BF)
    last.wait()
    branch = jnp.dot(ctx[...], wout[...], preferred_element_type=F32)
    floats = rows_ref[...].reshape(count * length, width).astype(F32)
    out_ref[...] = (floats + branch).astype(BF).reshape(count, length, width)


def encode(rows, gain, w_qkv, w_out):
    count, length, width = rows.shape
    tokens = count * length
    return pl.pallas_call(
        encode_kernel,
        out_shape=pltpu.VMEM(rows.shape, BF),
        in_specs=[VM, VM, ANY, ANY],
        out_specs=VM,
        scratch_shapes=[
            pltpu.VMEM((width, 3 * width), BF),
            pltpu.VMEM((width, width), BF),
            pltpu.VMEM((tokens, 3 * width), BF),
            pltpu.VMEM((tokens, width), BF),
            pltpu.SemaphoreType.DMA((13,)),
        ],
        compiler_params=pltpu.CompilerParams(vmem_limit_bytes=57 * MB),
        cost_estimate=cost(E_US),
        name="encode_rows",
    )(rows, gain, w_qkv, w_out)


def gather_rows(plan, sources, ids_ref, me, rows, slots, sems):
    bottom, top, plan = plan

    def look(s, found):
        code = ids_ref[s]
        owner, row = lax.shift_right_logical(code, 10), jnp.bitwise_and(code, PER - 1)
        hop = jnp.bitwise_xor(owner, me)
        inside = (hop >= bottom) & (hop < top)

        @pl.when(inside)
        def _():
            slots[found] = s
            for source, test, place in plan(sources, owner, hop, row):

                @pl.when(test)
                def _():
                    pltpu.make_async_copy(source.at[place], rows.at[found], sems.at[found]).start()

        return found + inside.astype(jnp.int32)

    return lax.fori_loop(0, ids_ref.shape[0], look, jnp.int32(0))


def project_groups(found, source, w_ref, rows, sems, finish):
    length, width = rows.shape[1:]
    chunk = 1024

    def arrive(i, carry):
        pltpu.make_async_copy(source.at[0], rows.at[i], sems.at[i]).wait()
        return carry

    def project(g, carry):
        i = GROUP * g
        lax.fori_loop(i, jnp.minimum(i + GROUP, found), arrive, 0)
        many = rows[pl.ds(i, GROUP)].reshape(GROUP * length, width)
        for b in range(w_ref.shape[1] // chunk):
            cols = pl.ds(b * chunk, chunk)
            out = jnp.dot(many, w_ref[:, cols], preferred_element_type=F32).astype(BF)
            for j in range(GROUP):
                finish(i + j, cols, out[j * length : (j + 1) * length])
        return carry

    lax.fori_loop(0, (found + GROUP - 1) // GROUP, project, 0)


def kv_kernel(plan, n_src, fresh, *refs):
    ids_ref, me_ref, w_in = refs[:3]
    sources = refs[3 : 3 + n_src]
    kv_hbm, w_ref, token_ref, rows, made, slots, sems, w_sem, out_sems = refs[-9:]
    if fresh:
        step = w_ref.shape[0] // 8
        loads = [
            pltpu.make_async_copy(w_in.at[0, pl.ds(i * step, step)], w_ref.at[pl.ds(i * step, step)], w_sem.at[i])
            for i in range(8)
        ]
        for load in loads:
            load.start()
    found = gather_rows(plan, sources, ids_ref, me_ref[0], rows, slots, sems)
    if fresh:
        for load in loads:
            load.wait()

    def store(i):
        return pltpu.make_async_copy(made.at[i], kv_hbm.at[slots[i]], out_sems.at[i])

    def send(i, cols):
        pltpu.make_async_copy(made.at[i, :, cols], kv_hbm.at[slots[i], :, cols], out_sems.at[i]).start()

    def finish(i, cols, part):
        made[i, :, cols] = part

        @pl.when(i < found)
        def _():
            send(i, cols)

    def drain(i, carry):
        store(i).wait()
        return carry

    project_groups(found, sources[0], w_ref, rows, sems, finish)
    lax.fori_loop(0, found, drain, 0)
    token_ref[...] = jnp.zeros_like(token_ref)


def keyvals_part(ids, me, sources, w_kv, before, plan, most):
    length, width = sources[0].shape[1:]
    features = w_kv.shape[-1]
    slots = ids.shape[0]
    most = -(-min(most, slots) // GROUP) * GROUP
    fresh = before is None
    operands = [ids, me, w_kv, *sources]
    specs = [SM, SM, ANY if fresh else VM] + [ANY] * len(sources)
    aliases = {}
    if not fresh:
        aliases = {2: 1, len(operands): 0}
        operands.append(before)
        specs.append(ANY)
    return pl.pallas_call(
        functools.partial(kv_kernel, plan, len(sources), fresh),
        out_shape=[
            jax.ShapeDtypeStruct((slots, length, features), BF),
            pltpu.VMEM((width, features), BF),
            pltpu.VMEM((8, 128), F32),
        ],
        in_specs=specs,
        out_specs=[ANY, VM, VM],
        input_output_aliases=aliases,
        scratch_shapes=[
            pltpu.VMEM((most, length, width), BF),
            pltpu.VMEM((most, length, features), BF),
            pltpu.SMEM((most,), jnp.int32),
            pltpu.SemaphoreType.DMA((most,)),
            pltpu.SemaphoreType.DMA((8,)),
            pltpu.SemaphoreType.DMA((most,)),
        ],
        compiler_params=pltpu.CompilerParams(vmem_limit_bytes=(48 if fresh else 44) * MB),
        cost_estimate=cost(KV_US),
        name="keyvals_rows",
    )(*operands)


def attend_span(span, queries, kv_ref, out_ref):
    width = queries.shape[1]
    picks, length = 2, kv_ref.shape[1]
    keys = picks * length
    lane = lax.broadcasted_iota(jnp.int32, (SPAN, 2 * HD), 1)
    first = lane < HD
    zero = jnp.zeros((SPAN, 2 * HD), BF)
    scale = LOG2E / math.sqrt(HD)
    pairs = width // (2 * HD)
    here = pl.ds(pl.multiple_of(span * SPAN, SPAN), SPAN)
    scores = []
    for h in range(pairs):
        cols = slice(h * 2 * HD, (h + 1) * 2 * HD)
        q = queries[here, cols]
        qq = jnp.concatenate([jnp.where(first, q, zero), jnp.where(first, zero, q)], axis=0)
        k = kv_ref[pl.ds(span * picks, picks), :, cols].reshape(keys, 2 * HD)
        scores.append(lax.dot_general(qq, k, (((1,), (1,)), ((), ())), preferred_element_type=F32))
    weights = []
    for part in scores:
        highest = jnp.max(part, axis=-1, keepdims=True)
        powers = jnp.exp2((part - highest) * scale)
        weights.append((powers.astype(BF), 1.0 / jnp.sum(powers, axis=-1, keepdims=True)))
    for h in range(pairs):
        cols = slice(h * 2 * HD, (h + 1) * 2 * HD)
        values = slice(width + h * 2 * HD, width + (h + 1) * 2 * HD)
        v = kv_ref[pl.ds(span * picks, picks), :, values].reshape(keys, 2 * HD)
        both = jnp.dot(weights[h][0], v, preferred_element_type=F32) * weights[h][1]
        out_ref[here, cols] = jnp.where(first, both[:SPAN], both[SPAN:]).astype(BF)


def last_kernel(plan, n_src, *refs):
    ids_ref, me_ref, w_ref = refs[:3]
    sources = refs[3 : 3 + n_src]
    made, rows, slots, sems = refs[3 + n_src :]
    found = gather_rows(plan, sources, ids_ref, me_ref[0], rows, slots, sems)

    def finish(i, cols, part):
        made[i, :, cols] = part

    project_groups(found, sources[0], w_ref, rows, sems, finish)


def last_keyvals(ids, me, sources, w, plan):
    length, width = sources[0].shape[1:]
    return pl.pallas_call(
        functools.partial(last_kernel, plan, len(sources)),
        out_shape=pltpu.VMEM((GROUP, length, w.shape[1]), BF),
        in_specs=[SM, SM, VM] + [ANY] * len(sources),
        out_specs=VM,
        scratch_shapes=[
            pltpu.VMEM((GROUP, length, width), BF),
            pltpu.SMEM((GROUP,), jnp.int32),
            pltpu.SemaphoreType.DMA((GROUP,)),
        ],
        compiler_params=pltpu.CompilerParams(vmem_limit_bytes=40 * MB),
        cost_estimate=cost(0.01),
        name="last_keyvals",
    )(ids, me, w, *sources)


def cross_kernel(bottom, *refs):
    ids_ref, me_ref, kv_hbm, q_hbm = refs[:4]
    made = refs[4] if len(refs) == 12 else None
    out_hbm, keyvals, queries, result, kv_sems, q_sems, out_sems = refs[-7:]
    tokens = queries.shape[0]
    total = ids_ref.shape[0]
    picks = total * SPAN // tokens
    spans = tokens // SPAN
    ahead = min(AHEAD, spans)

    def fetch(s):
        return pltpu.make_async_copy(kv_hbm.at[s], keyvals.at[s], kv_sems.at[s])

    def rows_of(span):
        return pl.ds(pl.multiple_of(span * SPAN, SPAN), SPAN)

    def load(span):
        here = rows_of(span)
        return pltpu.make_async_copy(q_hbm.at[0, here], queries.at[here], q_sems.at[span])

    def store(span):
        here = rows_of(span)
        return pltpu.make_async_copy(result.at[here], out_hbm.at[0, here], out_sems.at[span])

    def begin(span, found):
        load(span).start()
        for j in range(picks):
            s = span * picks + j
            if made is None:
                fetch(s).start()
                continue
            late = jnp.bitwise_xor(lax.shift_right_logical(ids_ref[s], 10), me_ref[0]) >= bottom

            @pl.when(late)
            def _():
                pltpu.make_async_copy(made.at[found], keyvals.at[s], kv_sems.at[s]).start()

            @pl.when(jnp.logical_not(late))
            def _():
                fetch(s).start()

            found = found + late.astype(jnp.int32)
        return found

    found = lax.fori_loop(0, ahead, begin, jnp.int32(0))

    def attend(span, found):
        found = lax.cond(span + ahead < spans, begin, lambda span, found: found, span + ahead, found)
        load(span).wait()
        for j in range(picks):
            fetch(span * picks + j).wait()
        attend_span(span, queries, keyvals, result)
        store(span).start()
        return found

    lax.fori_loop(0, spans, attend, found)

    def drain(span, carry):
        store(span).wait()
        return carry

    lax.fori_loop(0, tokens // SPAN, drain, 0)


def cross(ids, me, kv, queries, made, bottom):
    slots, length, both = kv.shape
    tokens, features = queries.shape[1:]
    extra = [] if made is None else [made]
    return pl.pallas_call(
        functools.partial(cross_kernel, bottom),
        out_shape=jax.ShapeDtypeStruct((1, tokens, features), BF),
        in_specs=[SM, SM, ANY, ANY] + [VM] * len(extra),
        out_specs=ANY,
        scratch_shapes=[
            pltpu.VMEM((slots, length, both), BF),
            pltpu.VMEM((tokens, features), BF),
            pltpu.VMEM((tokens, features), BF),
            pltpu.SemaphoreType.DMA((slots,)),
            pltpu.SemaphoreType.DMA((tokens // SPAN,)),
            pltpu.SemaphoreType.DMA((tokens // SPAN,)),
        ],
        compiler_params=pltpu.CompilerParams(vmem_limit_bytes=44 * MB),
        cost_estimate=cost(CROSS_US),
        name="cross_spans",
    )(ids, me, kv, queries, *extra)


def split_kernel(x_ref, y_ref, token_ref, low_ref, high_ref, x_out, y_out, sems):
    half = low_ref.shape[0]
    copies = [
        pltpu.make_async_copy(x_ref.at[pl.ds(0, half)], low_ref, sems.at[0]),
        pltpu.make_async_copy(y_ref.at[pl.ds(half, high_ref.shape[0])], high_ref, sems.at[1]),
    ]
    for copy in copies:
        copy.start()
    for copy in copies:
        copy.wait()


def split(x, y, token):
    half = x.shape[0] // 2
    return pl.pallas_call(
        split_kernel,
        out_shape=[
            pltpu.VMEM((half,) + x.shape[1:], BF),
            pltpu.VMEM((y.shape[0] - half,) + x.shape[1:], BF),
            jax.ShapeDtypeStruct(x.shape, BF),
            jax.ShapeDtypeStruct(y.shape, BF),
        ],
        in_specs=[ANY, ANY, VM],
        out_specs=[VM] * 2 + [ANY] * 2,
        input_output_aliases={0: 2, 1: 3},
        scratch_shapes=[pltpu.SemaphoreType.DMA((2,))],
        compiler_params=pltpu.CompilerParams(vmem_limit_bytes=24 * MB),
        cost_estimate=cost(0.1),
        name="next_sends",
    )(x, y, token)


def relay_kernel(low_ref, high_ref, token_ref, low_out, high_out):
    pass


def relay(low, high, token):
    return pl.pallas_call(
        relay_kernel,
        out_shape=[jax.ShapeDtypeStruct(low.shape, BF), jax.ShapeDtypeStruct(high.shape, BF)],
        in_specs=[ANY, ANY, VM],
        out_specs=[ANY, ANY],
        input_output_aliases={0: 0, 1: 1},
        compiler_params=pltpu.CompilerParams(vmem_limit_bytes=MB),
        cost_estimate=cost(0.1),
        name="after_rows",
    )(low, high, token)


def shifted(block):
    n = lax.axis_size("section")
    return lax.ppermute(block, "section", [((i - 1) % n, i) for i in range(n)])


def swapped(block, hop):
    n = lax.axis_size("dp")
    return lax.ppermute(block, "dp", [(i, i ^ hop) for i in range(n)])


def shards(query_states, cache_emb, nb_owner, nb_row, enc_gain, w_qkv, w_out, w_kv):
    dp = lax.axis_size("dp")
    slots = nb_owner.shape[1] * nb_owner.shape[2]
    per = cache_emb.shape[0]
    received = shifted(query_states)
    me = lax.axis_index("dp").astype(jnp.int32).reshape(1)
    ids = (nb_owner * PER + nb_row).reshape(-1)
    own = encode(cache_emb, enc_gain, w_qkv, w_out)
    part = functools.partial(keyvals_part, ids, me)
    if dp == 8 and per % 2 == 0:
        half = per // 2

        def nearest(src, owner, hop, row):
            return [(src[i], hop == i, row) for i in range(2)]

        def middle(src, owner, hop, row):
            return [(src[i], hop == i + 2, row) for i in range(4)]

        def last(src, owner, hop, row):
            lows = [(src[i], (hop == i + 6) & (row < half), row) for i in range(2)]
            return lows + [(src[i + 2], (hop == i + 6) & (row >= half), row - half) for i in range(2)]

        x, y, near = swapped(own, 2), swapped(own, 4), swapped(own, 1)
        kv, w, token = part([own, near], w_kv, None, (0, 2, nearest), 4)
        xl, yh, x, y = split(x, y, token)
        dl, dh = swapped(xl, 4), swapped(yh, 2)
        kv, w, token = part([x, swapped(x, 1), y, swapped(y, 1)], w, kv, (2, 6, middle), 8)
        dl, dh = relay(dl, dh, token)
        made = last_keyvals(ids, me, [dl, swapped(dl, 1), dh, swapped(dh, 1)], w, (6, 8, last))
    else:
        whole = lax.all_gather(own, "dp", axis=0, tiled=True)

        def everything(src, owner, hop, row):
            return [(src[0], owner >= 0, owner * per + row)]

        kv, w, _ = part([whole], w_kv, None, (0, 1 << 20, everything), slots)
        made = None
    return cross(ids, me, kv, received, made, 6)


def solution(mesh):
    placed = (
        P("section", "dp", None),
        P("dp", None, None),
        P("section", "dp", None),
        P("section", "dp", None),
        P("section", None),
        P("section", None, None),
        P("section", None, None),
        P("section", None, None),
    )
    return jax.shard_map(
        shards, mesh=mesh, in_specs=placed, out_specs=P("section", "dp", None), check_vma=False
    )
```

```python
import functools
import math

import jax
import jax.numpy as jnp
from jax import lax
from jax.experimental import pallas as pl
from jax.experimental.pallas import tpu as pltpu
from jax.sharding import PartitionSpec as P

HD = 128
ENC_HD = 64
SPAN = 64
LOG2E = 1.4426950408889634
BF = jnp.bfloat16
F32 = jnp.float32
MB = 2**20
ANY = pl.BlockSpec(memory_space=pl.ANY)
VM = pl.BlockSpec(memory_space=pltpu.VMEM)
SM = pl.BlockSpec(memory_space=pltpu.SMEM)
PER = 1024
GROUP = 4
AHEAD = 3
E_US, KV_US, CROSS_US = 8.0, 4.0, 6.0


def cost(us):
    return pl.CostEstimate(flops=int(us * 1.0e9), bytes_accessed=1, transcendentals=0)


def encode_kernel(
    rows_ref, gain_ref, wqkv_hbm, wout_hbm, out_ref, wqkv, wout, proj, ctx, sems
):
    count, length, width = rows_ref.shape
    step = width // 4
    pieces = [
        [
            pltpu.make_async_copy(
                wqkv_hbm.at[0, pl.ds(j * step, step), pl.ds(i * width, width)],
                wqkv.at[pl.ds(j * step, step), pl.ds(i * width, width)],
                sems.at[4 * i + j],
            )
            for j in range(4)
        ]
        for i in range(3)
    ]
    last = pltpu.make_async_copy(wout_hbm.at[0], wout, sems.at[12])
    for piece in pieces:
        for copy in piece:
            copy.start()
    last.start()
    tokens = rows_ref[...].reshape(count * length, width)
    floats = tokens.astype(F32)
    factor = lax.rsqrt(jnp.mean(floats * floats, axis=-1, keepdims=True) + 1e-06)
    ctx[...] = (floats * factor * gain_ref[...]).astype(BF)
    for i, piece in enumerate(pieces):
        for copy in piece:
            copy.wait()
        cols = slice(i * width, (i + 1) * width)
        proj[:, cols] = jnp.dot(ctx[...], wqkv[:, cols], preferred_element_type=F32).astype(BF)
    lane = lax.broadcasted_iota(jnp.int32, (length, 2 * ENC_HD), 1)
    first = lane < ENC_HD
    zero = jnp.zeros((length, 2 * ENC_HD), BF)
    scale = LOG2E / math.sqrt(ENC_HD)
    column = lax.broadcasted_iota(jnp.int32, (2 * length, 2 * length), 1)
    line = lax.broadcasted_iota(jnp.int32, (2 * length, 2 * length), 0)
    same = jnp.where((column < length) == (line < length), 1.0, 0.0).astype(BF)
    pairs = width // (2 * ENC_HD)
    for r in range(count):
        spot = slice(r * length, (r + 1) * length)

        def split(base):
            both = proj[spot, base : base + 2 * ENC_HD]
            return jnp.concatenate([jnp.where(first, both, zero), jnp.where(first, zero, both)], axis=0)

        scores = []
        for p in range(pairs):
            base = p * 2 * ENC_HD
            q2 = proj[spot, base : base + 2 * ENC_HD]
            scores.append(
                lax.dot_general(q2, split(width + base), (((1,), (1,)), ((), ())), preferred_element_type=F32)
            )
        powers = [jnp.exp2(part * scale) for part in scores]
        sums = [jnp.dot(part.astype(BF), same, preferred_element_type=F32) for part in powers]
        weights = [(part * (1.0 / total)).astype(BF) for part, total in zip(powers, sums)]
        for p in range(pairs):
            base = p * 2 * ENC_HD
            out = jnp.dot(weights[p], split(2 * width + base), preferred_element_type=F32)
            ctx[spot, base : base + 2 * ENC_HD] = out.astype(BF)
    last.wait()
    branch = jnp.dot(ctx[...], wout[...], preferred_element_type=F32)
    floats = rows_ref[...].reshape(count * length, width).astype(F32)
    out_ref[...] = (floats + branch).astype(BF).reshape(count, length, width)


def encode(rows, gain, w_qkv, w_out):
    count, length, width = rows.shape
    tokens = count * length
    return pl.pallas_call(
        encode_kernel,
        out_shape=pltpu.VMEM(rows.shape, BF),
        in_specs=[VM, VM, ANY, ANY],
        out_specs=VM,
        scratch_shapes=[
            pltpu.VMEM((width, 3 * width), BF),
            pltpu.VMEM((width, width), BF),
            pltpu.VMEM((tokens, 3 * width), BF),
            pltpu.VMEM((tokens, width), BF),
            pltpu.SemaphoreType.DMA((13,)),
        ],
        compiler_params=pltpu.CompilerParams(vmem_limit_bytes=57 * MB),
        cost_estimate=cost(E_US),
        name="encode_rows",
    )(rows, gain, w_qkv, w_out)


def gather_rows(plan, sources, ids_ref, me, rows, slots, sems):
    bottom, top, plan = plan

    def look(s, found):
        code = ids_ref[s]
        owner, row = lax.shift_right_logical(code, 10), jnp.bitwise_and(code, PER - 1)
        hop = jnp.bitwise_xor(owner, me)
        inside = (hop >= bottom) & (hop < top)

        @pl.when(inside)
        def _():
            slots[found] = s
            for source, test, place in plan(sources, owner, hop, row):

                @pl.when(test)
                def _():
                    pltpu.make_async_copy(source.at[place], rows.at[found], sems.at[found]).start()

        return found + inside.astype(jnp.int32)

    return lax.fori_loop(0, ids_ref.shape[0], look, jnp.int32(0))


def project_groups(found, source, w_ref, rows, sems, finish):
    length, width = rows.shape[1:]
    chunk = 1024

    def arrive(i, carry):
        pltpu.make_async_copy(source.at[0], rows.at[i], sems.at[i]).wait()
        return carry

    def project(g, carry):
        i = GROUP * g
        lax.fori_loop(i, jnp.minimum(i + GROUP, found), arrive, 0)
        many = rows[pl.ds(i, GROUP)].reshape(GROUP * length, width)
        for b in range(w_ref.shape[1] // chunk):
            cols = pl.ds(b * chunk, chunk)
            out = jnp.dot(many, w_ref[:, cols], preferred_element_type=F32).astype(BF)
            for j in range(GROUP):
                finish(i + j, cols, out[j * length : (j + 1) * length])
        return carry

    lax.fori_loop(0, (found + GROUP - 1) // GROUP, project, 0)


def kv_kernel(plan, n_src, fresh, *refs):
    ids_ref, me_ref, w_in = refs[:3]
    sources = refs[3 : 3 + n_src]
    kv_hbm, w_ref, token_ref, rows, made, slots, sems, w_sem, out_sems = refs[-9:]
    if fresh:
        step = w_ref.shape[0] // 8
        loads = [
            pltpu.make_async_copy(w_in.at[0, pl.ds(i * step, step)], w_ref.at[pl.ds(i * step, step)], w_sem.at[i])
            for i in range(8)
        ]
        for load in loads:
            load.start()
    found = gather_rows(plan, sources, ids_ref, me_ref[0], rows, slots, sems)
    if fresh:
        for load in loads:
            load.wait()

    def store(i):
        return pltpu.make_async_copy(made.at[i], kv_hbm.at[slots[i]], out_sems.at[i])

    def send(i, cols):
        pltpu.make_async_copy(made.at[i, :, cols], kv_hbm.at[slots[i], :, cols], out_sems.at[i]).start()

    def finish(i, cols, part):
        made[i, :, cols] = part

        @pl.when(i < found)
        def _():
            send(i, cols)

    def drain(i, carry):
        store(i).wait()
        return carry

    project_groups(found, sources[0], w_ref, rows, sems, finish)
    lax.fori_loop(0, found, drain, 0)
    token_ref[...] = jnp.zeros_like(token_ref)


def keyvals_part(ids, me, sources, w_kv, before, plan, most):
    length, width = sources[0].shape[1:]
    features = w_kv.shape[-1]
    slots = ids.shape[0]
    most = -(-min(most, slots) // GROUP) * GROUP
    fresh = before is None
    operands = [ids, me, w_kv, *sources]
    specs = [SM, SM, ANY if fresh else VM] + [ANY] * len(sources)
    aliases = {}
    if not fresh:
        aliases = {2: 1, len(operands): 0}
        operands.append(before)
        specs.append(ANY)
    return pl.pallas_call(
        functools.partial(kv_kernel, plan, len(sources), fresh),
        out_shape=[
            jax.ShapeDtypeStruct((slots, length, features), BF),
            pltpu.VMEM((width, features), BF),
            pltpu.VMEM((8, 128), F32),
        ],
        in_specs=specs,
        out_specs=[ANY, VM, VM],
        input_output_aliases=aliases,
        scratch_shapes=[
            pltpu.VMEM((most, length, width), BF),
            pltpu.VMEM((most, length, features), BF),
            pltpu.SMEM((most,), jnp.int32),
            pltpu.SemaphoreType.DMA((most,)),
            pltpu.SemaphoreType.DMA((8,)),
            pltpu.SemaphoreType.DMA((most,)),
        ],
        compiler_params=pltpu.CompilerParams(vmem_limit_bytes=(46 if fresh else 42) * MB),
        cost_estimate=cost(KV_US),
        name="keyvals_rows",
    )(*operands)


def attend_span(span, queries, kv_ref, out_ref):
    width = queries.shape[1]
    picks, length = 2, kv_ref.shape[1]
    keys = picks * length
    lane = lax.broadcasted_iota(jnp.int32, (SPAN, 2 * HD), 1)
    first = lane < HD
    zero = jnp.zeros((SPAN, 2 * HD), BF)
    scale = LOG2E / math.sqrt(HD)
    pairs = width // (2 * HD)
    here = pl.ds(pl.multiple_of(span * SPAN, SPAN), SPAN)
    scores = []
    for h in range(pairs):
        cols = slice(h * 2 * HD, (h + 1) * 2 * HD)
        q = queries[here, cols]
        qq = jnp.concatenate([jnp.where(first, q, zero), jnp.where(first, zero, q)], axis=0)
        k = kv_ref[pl.ds(span * picks, picks), :, cols].reshape(keys, 2 * HD)
        scores.append(lax.dot_general(qq, k, (((1,), (1,)), ((), ())), preferred_element_type=F32))
    weights = []
    for part in scores:
        highest = jnp.max(part, axis=-1, keepdims=True)
        powers = jnp.exp2((part - highest) * scale)
        weights.append((powers.astype(BF), 1.0 / jnp.sum(powers, axis=-1, keepdims=True)))
    for h in range(pairs):
        cols = slice(h * 2 * HD, (h + 1) * 2 * HD)
        values = slice(width + h * 2 * HD, width + (h + 1) * 2 * HD)
        v = kv_ref[pl.ds(span * picks, picks), :, values].reshape(keys, 2 * HD)
        both = jnp.dot(weights[h][0], v, preferred_element_type=F32) * weights[h][1]
        out_ref[here, cols] = jnp.where(first, both[:SPAN], both[SPAN:]).astype(BF)


def last_kernel(plan, n_src, *refs):
    ids_ref, me_ref, w_ref = refs[:3]
    sources = refs[3 : 3 + n_src]
    made, rows, slots, sems = refs[3 + n_src :]
    found = gather_rows(plan, sources, ids_ref, me_ref[0], rows, slots, sems)

    def finish(i, cols, part):
        made[i, :, cols] = part

    project_groups(found, sources[0], w_ref, rows, sems, finish)


def last_keyvals(ids, me, sources, w, plan):
    length, width = sources[0].shape[1:]
    return pl.pallas_call(
        functools.partial(last_kernel, plan, len(sources)),
        out_shape=pltpu.VMEM((GROUP, length, w.shape[1]), BF),
        in_specs=[SM, SM, VM] + [ANY] * len(sources),
        out_specs=VM,
        scratch_shapes=[
            pltpu.VMEM((GROUP, length, width), BF),
            pltpu.SMEM((GROUP,), jnp.int32),
            pltpu.SemaphoreType.DMA((GROUP,)),
        ],
        compiler_params=pltpu.CompilerParams(vmem_limit_bytes=40 * MB),
        cost_estimate=cost(0.01),
        name="last_keyvals",
    )(ids, me, w, *sources)


def cross_kernel(bottom, *refs):
    ids_ref, me_ref, kv_hbm, q_hbm = refs[:4]
    made = refs[4] if len(refs) == 12 else None
    out_hbm, keyvals, queries, result, kv_sems, q_sems, out_sems = refs[-7:]
    tokens = queries.shape[0]
    total = ids_ref.shape[0]
    picks = total * SPAN // tokens
    spans = tokens // SPAN
    ahead = min(AHEAD, spans)

    def fetch(s):
        return pltpu.make_async_copy(kv_hbm.at[s], keyvals.at[s], kv_sems.at[s])

    def rows_of(span):
        return pl.ds(pl.multiple_of(span * SPAN, SPAN), SPAN)

    def load(span):
        here = rows_of(span)
        return pltpu.make_async_copy(q_hbm.at[0, here], queries.at[here], q_sems.at[span])

    def store(span):
        here = rows_of(span)
        return pltpu.make_async_copy(result.at[here], out_hbm.at[0, here], out_sems.at[span])

    def begin(span, found):
        load(span).start()
        for j in range(picks):
            s = span * picks + j
            if made is None:
                fetch(s).start()
                continue
            late = jnp.bitwise_xor(lax.shift_right_logical(ids_ref[s], 10), me_ref[0]) >= bottom

            @pl.when(late)
            def _():
                pltpu.make_async_copy(made.at[found], keyvals.at[s], kv_sems.at[s]).start()

            @pl.when(jnp.logical_not(late))
            def _():
                fetch(s).start()

            found = found + late.astype(jnp.int32)
        return found

    found = lax.fori_loop(0, ahead, begin, jnp.int32(0))

    def attend(span, found):
        found = lax.cond(span + ahead < spans, begin, lambda span, found: found, span + ahead, found)
        load(span).wait()
        for j in range(picks):
            fetch(span * picks + j).wait()
        attend_span(span, queries, keyvals, result)
        store(span).start()
        return found

    lax.fori_loop(0, spans, attend, found)

    def drain(span, carry):
        store(span).wait()
        return carry

    lax.fori_loop(0, tokens // SPAN, drain, 0)


def cross(ids, me, kv, queries, made, bottom):
    slots, length, both = kv.shape
    tokens, features = queries.shape[1:]
    extra = [] if made is None else [made]
    return pl.pallas_call(
        functools.partial(cross_kernel, bottom),
        out_shape=jax.ShapeDtypeStruct((1, tokens, features), BF),
        in_specs=[SM, SM, ANY, ANY] + [VM] * len(extra),
        out_specs=ANY,
        scratch_shapes=[
            pltpu.VMEM((slots, length, both), BF),
            pltpu.VMEM((tokens, features), BF),
            pltpu.VMEM((tokens, features), BF),
            pltpu.SemaphoreType.DMA((slots,)),
            pltpu.SemaphoreType.DMA((tokens // SPAN,)),
            pltpu.SemaphoreType.DMA((tokens // SPAN,)),
        ],
        compiler_params=pltpu.CompilerParams(vmem_limit_bytes=44 * MB),
        cost_estimate=cost(CROSS_US),
        name="cross_spans",
    )(ids, me, kv, queries, *extra)


def split_kernel(x_ref, y_ref, token_ref, low_ref, high_ref, x_out, y_out, sems):
    half = low_ref.shape[0]
    copies = [
        pltpu.make_async_copy(x_ref.at[pl.ds(0, half)], low_ref, sems.at[0]),
        pltpu.make_async_copy(y_ref.at[pl.ds(half, high_ref.shape[0])], high_ref, sems.at[1]),
    ]
    for copy in copies:
        copy.start()
    for copy in copies:
        copy.wait()


def split(x, y, token):
    half = x.shape[0] // 2
    return pl.pallas_call(
        split_kernel,
        out_shape=[
            pltpu.VMEM((half,) + x.shape[1:], BF),
            pltpu.VMEM((y.shape[0] - half,) + x.shape[1:], BF),
            jax.ShapeDtypeStruct(x.shape, BF),
            jax.ShapeDtypeStruct(y.shape, BF),
        ],
        in_specs=[ANY, ANY, VM],
        out_specs=[VM] * 2 + [ANY] * 2,
        input_output_aliases={0: 2, 1: 3},
        scratch_shapes=[pltpu.SemaphoreType.DMA((2,))],
        compiler_params=pltpu.CompilerParams(vmem_limit_bytes=24 * MB),
        cost_estimate=cost(0.1),
        name="next_sends",
    )(x, y, token)


def relay_kernel(low_ref, high_ref, token_ref, low_out, high_out):
    pass


def relay(low, high, token):
    return pl.pallas_call(
        relay_kernel,
        out_shape=[jax.ShapeDtypeStruct(low.shape, BF), jax.ShapeDtypeStruct(high.shape, BF)],
        in_specs=[ANY, ANY, VM],
        out_specs=[ANY, ANY],
        input_output_aliases={0: 0, 1: 1},
        compiler_params=pltpu.CompilerParams(vmem_limit_bytes=MB),
        cost_estimate=cost(0.1),
        name="after_rows",
    )(low, high, token)


def shifted(block):
    n = lax.axis_size("section")
    return lax.ppermute(block, "section", [((i - 1) % n, i) for i in range(n)])


def swapped(block, hop):
    n = lax.axis_size("dp")
    return lax.ppermute(block, "dp", [(i, i ^ hop) for i in range(n)])


def shards(query_states, cache_emb, nb_owner, nb_row, enc_gain, w_qkv, w_out, w_kv):
    dp = lax.axis_size("dp")
    slots = nb_owner.shape[1] * nb_owner.shape[2]
    per = cache_emb.shape[0]
    received = shifted(query_states)
    me = lax.axis_index("dp").astype(jnp.int32).reshape(1)
    ids = (nb_owner * PER + nb_row).reshape(-1)
    own = encode(cache_emb, enc_gain, w_qkv, w_out)
    part = functools.partial(keyvals_part, ids, me)
    if dp == 8 and per % 2 == 0:
        half = per // 2

        def nearest(src, owner, hop, row):
            return [(src[i], hop == i, row) for i in range(2)]

        def middle(src, owner, hop, row):
            return [(src[i], hop == i + 2, row) for i in range(4)]

        def last(src, owner, hop, row):
            lows = [(src[i], (hop == i + 6) & (row < half), row) for i in range(2)]
            return lows + [(src[i + 2], (hop == i + 6) & (row >= half), row - half) for i in range(2)]

        x, y, near = swapped(own, 2), swapped(own, 4), swapped(own, 1)
        kv, w, token = part([own, near], w_kv, None, (0, 2, nearest), 4)
        xl, yh, x, y = split(x, y, token)
        dl, dh = swapped(xl, 4), swapped(yh, 2)
        kv, w, token = part([x, swapped(x, 1), y, swapped(y, 1)], w, kv, (2, 6, middle), 8)
        dl, dh = relay(dl, dh, token)
        made = last_keyvals(ids, me, [dl, swapped(dl, 1), dh, swapped(dh, 1)], w, (6, 8, last))
    else:
        whole = lax.all_gather(own, "dp", axis=0, tiled=True)

        def everything(src, owner, hop, row):
            return [(src[0], owner >= 0, owner * per + row)]

        kv, w, _ = part([whole], w_kv, None, (0, 1 << 20, everything), slots)
        made = None
    return cross(ids, me, kv, received, made, 6)


def solution(mesh):
    placed = (
        P("section", "dp", None),
        P("dp", None, None),
        P("section", "dp", None),
        P("section", "dp", None),
        P("section", None),
        P("section", None, None),
        P("section", None, None),
        P("section", None, None),
    )
    return jax.shard_map(
        shards, mesh=mesh, in_specs=placed, out_specs=P("section", "dp", None), check_vma=False
    )
```

```python
import functools
import math

import jax
import jax.numpy as jnp
from jax import lax
from jax.experimental import pallas as pl
from jax.experimental.pallas import tpu as pltpu
from jax.sharding import PartitionSpec as P

HD = 128
ENC_HD = 64
SPAN = 64
LOG2E = 1.4426950408889634
BF = jnp.bfloat16
F32 = jnp.float32
MB = 2**20
ANY = pl.BlockSpec(memory_space=pl.ANY)
VM = pl.BlockSpec(memory_space=pltpu.VMEM)
SM = pl.BlockSpec(memory_space=pltpu.SMEM)
PER = 1024
GROUP = 4
AHEAD = 4
E_US, KV_US, CROSS_US = 8.0, 4.0, 6.0


def cost(us):
    return pl.CostEstimate(flops=int(us * 1.0e9), bytes_accessed=1, transcendentals=0)


def encode_kernel(
    rows_hbm, gain_ref, wqkv_hbm, wout_hbm, out_ref, rows_ref, wqkv, wout, proj, ctx, sems
):
    count, length, width = rows_ref.shape
    load = pltpu.make_async_copy(rows_hbm, rows_ref, sems.at[13])
    load.start()
    step = width // 4
    pieces = [
        [
            pltpu.make_async_copy(
                wqkv_hbm.at[0, pl.ds(j * step, step), pl.ds(i * width, width)],
                wqkv.at[pl.ds(j * step, step), pl.ds(i * width, width)],
                sems.at[4 * i + j],
            )
            for j in range(4)
        ]
        for i in range(3)
    ]
    last = pltpu.make_async_copy(wout_hbm.at[0], wout, sems.at[12])
    for piece in pieces:
        for copy in piece:
            copy.start()
    last.start()
    load.wait()
    tokens = rows_ref[...].reshape(count * length, width)
    floats = tokens.astype(F32)
    factor = lax.rsqrt(jnp.mean(floats * floats, axis=-1, keepdims=True) + 1e-06)
    ctx[...] = (floats * factor * gain_ref[...]).astype(BF)
    for i, piece in enumerate(pieces):
        for copy in piece:
            copy.wait()
        cols = slice(i * width, (i + 1) * width)
        proj[:, cols] = jnp.dot(ctx[...], wqkv[:, cols], preferred_element_type=F32).astype(BF)
    lane = lax.broadcasted_iota(jnp.int32, (length, 2 * ENC_HD), 1)
    first = lane < ENC_HD
    zero = jnp.zeros((length, 2 * ENC_HD), BF)
    scale = LOG2E / math.sqrt(ENC_HD)
    column = lax.broadcasted_iota(jnp.int32, (2 * length, 2 * length), 1)
    line = lax.broadcasted_iota(jnp.int32, (2 * length, 2 * length), 0)
    same = jnp.where((column < length) == (line < length), 1.0, 0.0).astype(BF)
    pairs = width // (2 * ENC_HD)
    for r in range(count):
        spot = slice(r * length, (r + 1) * length)

        def split(base):
            both = proj[spot, base : base + 2 * ENC_HD]
            return jnp.concatenate([jnp.where(first, both, zero), jnp.where(first, zero, both)], axis=0)

        scores = []
        for p in range(pairs):
            base = p * 2 * ENC_HD
            q2 = proj[spot, base : base + 2 * ENC_HD]
            scores.append(
                lax.dot_general(q2, split(width + base), (((1,), (1,)), ((), ())), preferred_element_type=F32)
            )
        powers = [jnp.exp2(part * scale) for part in scores]
        sums = [jnp.dot(part.astype(BF), same, preferred_element_type=F32) for part in powers]
        weights = [(part * (1.0 / total)).astype(BF) for part, total in zip(powers, sums)]
        for p in range(pairs):
            base = p * 2 * ENC_HD
            out = jnp.dot(weights[p], split(2 * width + base), preferred_element_type=F32)
            ctx[spot, base : base + 2 * ENC_HD] = out.astype(BF)
    last.wait()
    branch = jnp.dot(ctx[...], wout[...], preferred_element_type=F32)
    floats = rows_ref[...].reshape(count * length, width).astype(F32)
    out_ref[...] = (floats + branch).astype(BF).reshape(count, length, width)


def encode(rows, gain, w_qkv, w_out):
    count, length, width = rows.shape
    tokens = count * length
    return pl.pallas_call(
        encode_kernel,
        out_shape=pltpu.VMEM(rows.shape, BF),
        in_specs=[ANY, VM, ANY, ANY],
        out_specs=VM,
        scratch_shapes=[
            pltpu.VMEM(rows.shape, BF),
            pltpu.VMEM((width, 3 * width), BF),
            pltpu.VMEM((width, width), BF),
            pltpu.VMEM((tokens, 3 * width), BF),
            pltpu.VMEM((tokens, width), BF),
            pltpu.SemaphoreType.DMA((14,)),
        ],
        compiler_params=pltpu.CompilerParams(vmem_limit_bytes=57 * MB),
        cost_estimate=cost(E_US),
        name="encode_rows",
    )(rows, gain, w_qkv, w_out)


def gather_rows(plan, sources, ids_ref, me, rows, slots, sems):
    bottom, top, plan = plan

    def look(s, found):
        code = ids_ref[s]
        owner, row = lax.shift_right_logical(code, 10), jnp.bitwise_and(code, PER - 1)
        hop = jnp.bitwise_xor(owner, me)
        inside = (hop >= bottom) & (hop < top)

        @pl.when(inside)
        def _():
            slots[found] = s
            for source, test, place in plan(sources, owner, hop, row):

                @pl.when(test)
                def _():
                    pltpu.make_async_copy(source.at[place], rows.at[found], sems.at[found]).start()

        return found + inside.astype(jnp.int32)

    return lax.fori_loop(0, ids_ref.shape[0], look, jnp.int32(0))


def project_groups(found, source, w_ref, rows, sems, finish):
    length, width = rows.shape[1:]
    chunk = 1024

    def arrive(i, carry):
        pltpu.make_async_copy(source.at[0], rows.at[i], sems.at[i]).wait()
        return carry

    def project(g, carry):
        i = GROUP * g
        lax.fori_loop(i, jnp.minimum(i + GROUP, found), arrive, 0)
        many = rows[pl.ds(i, GROUP)].reshape(GROUP * length, width)
        for b in range(w_ref.shape[1] // chunk):
            cols = pl.ds(b * chunk, chunk)
            out = jnp.dot(many, w_ref[:, cols], preferred_element_type=F32).astype(BF)
            for j in range(GROUP):
                finish(i + j, cols, out[j * length : (j + 1) * length])
        return carry

    lax.fori_loop(0, (found + GROUP - 1) // GROUP, project, 0)


def kv_kernel(plan, n_src, fresh, *refs):
    ids_ref, me_ref, w_in = refs[:3]
    sources = refs[3 : 3 + n_src]
    kv_hbm, w_ref, token_ref, rows, made, slots, sems, w_sem, out_sems = refs[-9:]
    if fresh:
        step = w_ref.shape[0] // 8
        loads = [
            pltpu.make_async_copy(w_in.at[0, pl.ds(i * step, step)], w_ref.at[pl.ds(i * step, step)], w_sem.at[i])
            for i in range(8)
        ]
        for load in loads:
            load.start()
    found = gather_rows(plan, sources, ids_ref, me_ref[0], rows, slots, sems)
    if fresh:
        for load in loads:
            load.wait()

    def store(i):
        return pltpu.make_async_copy(made.at[i], kv_hbm.at[slots[i]], out_sems.at[i])

    def send(i, cols):
        pltpu.make_async_copy(made.at[i, :, cols], kv_hbm.at[slots[i], :, cols], out_sems.at[i]).start()

    def finish(i, cols, part):
        made[i, :, cols] = part

        @pl.when(i < found)
        def _():
            send(i, cols)

    def drain(i, carry):
        store(i).wait()
        return carry

    project_groups(found, sources[0], w_ref, rows, sems, finish)
    lax.fori_loop(0, found, drain, 0)
    token_ref[...] = jnp.zeros_like(token_ref)


def keyvals_part(ids, me, sources, w_kv, before, plan, most):
    length, width = sources[0].shape[1:]
    features = w_kv.shape[-1]
    slots = ids.shape[0]
    most = -(-min(most, slots) // GROUP) * GROUP
    fresh = before is None
    operands = [ids, me, w_kv, *sources]
    specs = [SM, SM, ANY if fresh else VM] + [ANY] * len(sources)
    aliases = {}
    if not fresh:
        aliases = {2: 1, len(operands): 0}
        operands.append(before)
        specs.append(ANY)
    return pl.pallas_call(
        functools.partial(kv_kernel, plan, len(sources), fresh),
        out_shape=[
            jax.ShapeDtypeStruct((slots, length, features), BF),
            pltpu.VMEM((width, features), BF),
            pltpu.VMEM((8, 128), F32),
        ],
        in_specs=specs,
        out_specs=[ANY, VM, VM],
        input_output_aliases=aliases,
        scratch_shapes=[
            pltpu.VMEM((most, length, width), BF),
            pltpu.VMEM((most, length, features), BF),
            pltpu.SMEM((most,), jnp.int32),
            pltpu.SemaphoreType.DMA((most,)),
            pltpu.SemaphoreType.DMA((8,)),
            pltpu.SemaphoreType.DMA((most,)),
        ],
        compiler_params=pltpu.CompilerParams(vmem_limit_bytes=(46 if fresh else 42) * MB),
        cost_estimate=cost(KV_US),
        name="keyvals_rows",
    )(*operands)


def attend_span(span, queries, kv_ref, out_ref):
    width = queries.shape[1]
    picks, length = 2, kv_ref.shape[1]
    keys = picks * length
    lane = lax.broadcasted_iota(jnp.int32, (SPAN, 2 * HD), 1)
    first = lane < HD
    zero = jnp.zeros((SPAN, 2 * HD), BF)
    scale = LOG2E / math.sqrt(HD)
    pairs = width // (2 * HD)
    here = pl.ds(pl.multiple_of(span * SPAN, SPAN), SPAN)
    scores = []
    for h in range(pairs):
        cols = slice(h * 2 * HD, (h + 1) * 2 * HD)
        q = queries[here, cols]
        qq = jnp.concatenate([jnp.where(first, q, zero), jnp.where(first, zero, q)], axis=0)
        k = kv_ref[pl.ds(span * picks, picks), :, cols].reshape(keys, 2 * HD)
        scores.append(lax.dot_general(qq, k, (((1,), (1,)), ((), ())), preferred_element_type=F32))
    weights = []
    for part in scores:
        highest = jnp.max(part, axis=-1, keepdims=True)
        powers = jnp.exp2((part - highest) * scale)
        weights.append((powers.astype(BF), 1.0 / jnp.sum(powers, axis=-1, keepdims=True)))
    for h in range(pairs):
        cols = slice(h * 2 * HD, (h + 1) * 2 * HD)
        values = slice(width + h * 2 * HD, width + (h + 1) * 2 * HD)
        v = kv_ref[pl.ds(span * picks, picks), :, values].reshape(keys, 2 * HD)
        both = jnp.dot(weights[h][0], v, preferred_element_type=F32) * weights[h][1]
        out_ref[here, cols] = jnp.where(first, both[:SPAN], both[SPAN:]).astype(BF)


def last_kernel(plan, n_src, *refs):
    ids_ref, me_ref, w_ref = refs[:3]
    sources = refs[3 : 3 + n_src]
    made, rows, slots, sems = refs[3 + n_src :]
    found = gather_rows(plan, sources, ids_ref, me_ref[0], rows, slots, sems)

    def finish(i, cols, part):
        made[i, :, cols] = part

    project_groups(found, sources[0], w_ref, rows, sems, finish)


def last_keyvals(ids, me, sources, w, plan):
    length, width = sources[0].shape[1:]
    return pl.pallas_call(
        functools.partial(last_kernel, plan, len(sources)),
        out_shape=pltpu.VMEM((GROUP, length, w.shape[1]), BF),
        in_specs=[SM, SM, VM] + [ANY] * len(sources),
        out_specs=VM,
        scratch_shapes=[
            pltpu.VMEM((GROUP, length, width), BF),
            pltpu.SMEM((GROUP,), jnp.int32),
            pltpu.SemaphoreType.DMA((GROUP,)),
        ],
        compiler_params=pltpu.CompilerParams(vmem_limit_bytes=40 * MB),
        cost_estimate=cost(0.01),
        name="last_keyvals",
    )(ids, me, w, *sources)


def cross_kernel(bottom, *refs):
    ids_ref, me_ref, kv_hbm, q_hbm = refs[:4]
    made = refs[4] if len(refs) == 12 else None
    out_hbm, keyvals, queries, result, kv_sems, q_sems, out_sems = refs[-7:]
    tokens = queries.shape[0]
    total = ids_ref.shape[0]
    picks = total * SPAN // tokens
    spans = tokens // SPAN
    ahead = min(AHEAD, spans)

    def fetch(s):
        return pltpu.make_async_copy(kv_hbm.at[s], keyvals.at[s], kv_sems.at[s])

    def rows_of(span):
        return pl.ds(pl.multiple_of(span * SPAN, SPAN), SPAN)

    def load(span):
        here = rows_of(span)
        return pltpu.make_async_copy(q_hbm.at[0, here], queries.at[here], q_sems.at[span])

    def store(span):
        here = rows_of(span)
        return pltpu.make_async_copy(result.at[here], out_hbm.at[0, here], out_sems.at[span])

    def begin(span, found):
        load(span).start()
        for j in range(picks):
            s = span * picks + j
            if made is None:
                fetch(s).start()
                continue
            late = jnp.bitwise_xor(lax.shift_right_logical(ids_ref[s], 10), me_ref[0]) >= bottom

            @pl.when(late)
            def _():
                pltpu.make_async_copy(made.at[found], keyvals.at[s], kv_sems.at[s]).start()

            @pl.when(jnp.logical_not(late))
            def _():
                fetch(s).start()

            found = found + late.astype(jnp.int32)
        return found

    found = lax.fori_loop(0, ahead, begin, jnp.int32(0))

    def attend(span, found):
        found = lax.cond(span + ahead < spans, begin, lambda span, found: found, span + ahead, found)
        load(span).wait()
        for j in range(picks):
            fetch(span * picks + j).wait()
        attend_span(span, queries, keyvals, result)
        store(span).start()
        return found

    lax.fori_loop(0, spans, attend, found)

    def drain(span, carry):
        store(span).wait()
        return carry

    lax.fori_loop(0, tokens // SPAN, drain, 0)


def cross(ids, me, kv, queries, made, bottom):
    slots, length, both = kv.shape
    tokens, features = queries.shape[1:]
    extra = [] if made is None else [made]
    return pl.pallas_call(
        functools.partial(cross_kernel, bottom),
        out_shape=jax.ShapeDtypeStruct((1, tokens, features), BF),
        in_specs=[SM, SM, ANY, ANY] + [VM] * len(extra),
        out_specs=ANY,
        scratch_shapes=[
            pltpu.VMEM((slots, length, both), BF),
            pltpu.VMEM((tokens, features), BF),
            pltpu.VMEM((tokens, features), BF),
            pltpu.SemaphoreType.DMA((slots,)),
            pltpu.SemaphoreType.DMA((tokens // SPAN,)),
            pltpu.SemaphoreType.DMA((tokens // SPAN,)),
        ],
        compiler_params=pltpu.CompilerParams(vmem_limit_bytes=44 * MB),
        cost_estimate=cost(CROSS_US),
        name="cross_spans",
    )(ids, me, kv, queries, *extra)


def split_kernel(x_ref, y_ref, token_ref, low_ref, high_ref, x_out, y_out, sems):
    half = low_ref.shape[0]
    copies = [
        pltpu.make_async_copy(x_ref.at[pl.ds(0, half)], low_ref, sems.at[0]),
        pltpu.make_async_copy(y_ref.at[pl.ds(half, high_ref.shape[0])], high_ref, sems.at[1]),
    ]
    for copy in copies:
        copy.start()
    for copy in copies:
        copy.wait()


def split(x, y, token):
    half = x.shape[0] // 2
    return pl.pallas_call(
        split_kernel,
        out_shape=[
            pltpu.VMEM((half,) + x.shape[1:], BF),
            pltpu.VMEM((y.shape[0] - half,) + x.shape[1:], BF),
            jax.ShapeDtypeStruct(x.shape, BF),
            jax.ShapeDtypeStruct(y.shape, BF),
        ],
        in_specs=[ANY, ANY, VM],
        out_specs=[VM] * 2 + [ANY] * 2,
        input_output_aliases={0: 2, 1: 3},
        scratch_shapes=[pltpu.SemaphoreType.DMA((2,))],
        compiler_params=pltpu.CompilerParams(vmem_limit_bytes=24 * MB),
        cost_estimate=cost(0.1),
        name="next_sends",
    )(x, y, token)


def relay_kernel(low_ref, high_ref, token_ref, low_out, high_out):
    pass


def relay(low, high, token):
    return pl.pallas_call(
        relay_kernel,
        out_shape=[jax.ShapeDtypeStruct(low.shape, BF), jax.ShapeDtypeStruct(high.shape, BF)],
        in_specs=[ANY, ANY, VM],
        out_specs=[ANY, ANY],
        input_output_aliases={0: 0, 1: 1},
        compiler_params=pltpu.CompilerParams(vmem_limit_bytes=MB),
        cost_estimate=cost(0.1),
        name="after_rows",
    )(low, high, token)


def shifted(block):
    n = lax.axis_size("section")
    return lax.ppermute(block, "section", [((i - 1) % n, i) for i in range(n)])


def swapped(block, hop):
    n = lax.axis_size("dp")
    return lax.ppermute(block, "dp", [(i, i ^ hop) for i in range(n)])


def shards(query_states, cache_emb, nb_owner, nb_row, enc_gain, w_qkv, w_out, w_kv):
    dp = lax.axis_size("dp")
    slots = nb_owner.shape[1] * nb_owner.shape[2]
    per = cache_emb.shape[0]
    received = shifted(query_states)
    me = lax.axis_index("dp").astype(jnp.int32).reshape(1)
    ids = (nb_owner * PER + nb_row).reshape(-1)
    own = encode(cache_emb, enc_gain, w_qkv, w_out)
    part = functools.partial(keyvals_part, ids, me)
    if dp == 8 and per % 2 == 0:
        half = per // 2

        def nearest(src, owner, hop, row):
            return [(src[i], hop == i, row) for i in range(2)]

        def middle(src, owner, hop, row):
            return [(src[i], hop == i + 2, row) for i in range(4)]

        def last(src, owner, hop, row):
            lows = [(src[i], (hop == i + 6) & (row < half), row) for i in range(2)]
            return lows + [(src[i + 2], (hop == i + 6) & (row >= half), row - half) for i in range(2)]

        x, y, near = swapped(own, 2), swapped(own, 4), swapped(own, 1)
        kv, w, token = part([own, near], w_kv, None, (0, 2, nearest), 4)
        xl, yh, x, y = split(x, y, token)
        dl, dh = swapped(xl, 4), swapped(yh, 2)
        kv, w, token = part([x, swapped(x, 1), y, swapped(y, 1)], w, kv, (2, 6, middle), 8)
        dl, dh = relay(dl, dh, token)
        made = last_keyvals(ids, me, [dl, swapped(dl, 1), dh, swapped(dh, 1)], w, (6, 8, last))
    else:
        whole = lax.all_gather(own, "dp", axis=0, tiled=True)

        def everything(src, owner, hop, row):
            return [(src[0], owner >= 0, owner * per + row)]

        kv, w, _ = part([whole], w_kv, None, (0, 1 << 20, everything), slots)
        made = None
    return cross(ids, me, kv, received, made, 6)


def solution(mesh):
    placed = (
        P("section", "dp", None),
        P("dp", None, None),
        P("section", "dp", None),
        P("section", "dp", None),
        P("section", None),
        P("section", None, None),
        P("section", None, None),
        P("section", None, None),
    )
    return jax.shard_map(
        shards, mesh=mesh, in_specs=placed, out_specs=P("section", "dp", None), check_vma=False
    )
```
